128 devices in a mesh: pix: 8 (over z, core), date: 16 (over y, x).
Axes of the slice: x: 4, y: 4, z: 4, core: 2. Of those that a mesh axis runs over, the one named last changes fastest.
Arguments:
- acquisitions: float32 [2, 288, 32, 1024], P(None, 'date', None, 'pix')
- offsets: int32 [288, 3], P('date'), may hold values from 1 to 4, as said below
Outputs:
- coherence: float32 [288, 3, 32, 1024], P(None, None, 'date', 'pix')
- displacement: float32 [288, 32, 1024], P(None, 'date', 'pix')
The draws below stay inside these ranges and needn't reach their ends.
Inputs may be any that keep to these rules, and one draw needn't show every extreme that they name: Each row holds 3 distinct offsets, one of them always 4.
All inputs are finite; a program needn't handle non-finite values.
Results may differ from the reference program's by a relative error of at most 0.0001.
Values sent between devices are 32-bit elements; how exact they have to be, the bound alone decides.
No kernel may reach another device: no remote copies, remote signals or barrier semaphores. Data moves between devices by JAX's collectives and lax.ppermute only.
A program may use at most 64 MiB of HBM per device.

```python
import jax
import jax.numpy as jnp
from jax import lax

DATES = 288
ROWS = 32
COLS = 1024
SPAN = 4
K = 3
HR = 2
HC = 7
ITERS = 6


def draw_acquisitions(key, part):
    key = jax.random.fold_in(key, 11)
    keys = jax.random.split(key, 6)
    common_real = jax.random.normal(keys[0], (ROWS, COLS), jnp.float32)
    common_imag = jax.random.normal(keys[1], (ROWS, COLS), jnp.float32)
    texture = jax.random.uniform(keys[2], (ROWS, COLS), jnp.float32, -1.0, 1.0)
    drift = jax.random.uniform(keys[3], (DATES, 1, 1), jnp.float32, -3.0, 3.0)
    noise_real = 0.6 * jax.random.normal(keys[4], (DATES, ROWS, COLS), jnp.float32)
    noise_imag = 0.6 * jax.random.normal(keys[5], (DATES, ROWS, COLS), jnp.float32)
    phase = drift * texture
    cosine = jnp.cos(phase)
    sine = jnp.sin(phase)
    real_part = common_real * cosine - common_imag * sine + noise_real
    imag_part = common_real * sine + common_imag * cosine + noise_imag
    return jnp.stack([real_part, imag_part]).astype(jnp.float32)


def draw_offsets(key, part):
    key = jax.random.fold_in(key, 23)
    keys = jax.random.split(key, DATES)
    chosen = jax.vmap(lambda k: jax.random.permutation(k, SPAN - 1)[:K - 1] + 1)(keys)
    longest = jnp.full((DATES, 1), SPAN, jnp.int32)
    return jnp.concatenate([chosen.astype(jnp.int32), longest], axis=1).astype(jnp.int32)


def setup_inputs(seed: int = 0) -> dict:
    seeds = jax.random.split(jax.random.key(seed), 3)
    acquisitions = draw_acquisitions(jax.random.fold_in(seeds[2], 71), 0)
    offsets = draw_offsets(jax.random.fold_in(seeds[2], 71), 0)
    return {"acquisitions": acquisitions, "offsets": offsets}


DAMPING = 0.05
EPSILON = 1e-06

def box_sum(field, row_pad):
    if row_pad:
        widths = [(0, 0)] * (field.ndim - 2) + [(HR, HR), (0, 0)]
        field = jnp.pad(field, widths)
    span_cols = field.shape[-1] - 2 * HC
    total = field[..., 0:span_cols]
    for t in range(1, 2 * HC + 1):
        total = total + field[..., t:t + span_cols]
    span_rows = field.shape[-2] - 2 * HR
    result = total[..., 0:span_rows, :]
    for t in range(1, 2 * HR + 1):
        result = result + total[..., t:t + span_rows, :]
    return result

def pair_stats(extended, offsets, usable, ref_count, row_pad):
    powers = box_sum(extended[0] * extended[0] + extended[1] * extended[1], row_pad)
    real_ref = extended[0, :ref_count]
    imag_ref = extended[1, :ref_count]
    coherence_list = []
    sine_list = []
    for k in range(K):
        second = jnp.minimum(jnp.arange(ref_count, dtype=jnp.int32) + offsets[:, k], extended.shape[1] - 1).astype(jnp.int32)
        partner = jnp.take(extended, second, axis=1)
        looked_real = box_sum(real_ref * partner[0] + imag_ref * partner[1], row_pad)
        looked_imag = box_sum(imag_ref * partner[0] - real_ref * partner[1], row_pad)
        denominator = jnp.sqrt(powers[:ref_count] * jnp.take(powers, second, axis=0) + EPSILON)
        weight = usable[:, k][:, None, None]
        coherence_list.append(weight * jnp.sqrt(looked_real * looked_real + looked_imag * looked_imag) / denominator)
        sine_list.append(weight * looked_imag / denominator)
    return (jnp.stack(coherence_list, axis=1), jnp.stack(sine_list, axis=1))

def solve(coherence, sine_part, offsets):
    trailing = coherence.ndim - 2
    selectors = [(offsets == s).astype(jnp.float32).reshape(offsets.shape + (1,) * trailing) for s in range(1, SPAN + 1)]

    def later_values(field, s):
        return jnp.concatenate([field[s:], jnp.zeros_like(field[:s])], axis=0)

    def earlier_values(field, s):
        return jnp.concatenate([jnp.zeros_like(field[:s]), field[:-s]], axis=0)

    def forward(field):
        partner = selectors[0] * later_values(field, 1)[:, None]
        for s in range(2, SPAN + 1):
            partner = partner + selectors[s - 1] * later_values(field, s)[:, None]
        return partner - field[:, None]

    def backward(values):
        result = -lax.optimization_barrier(jnp.sum(values, axis=1))
        for s in range(1, SPAN + 1):
            result = result + earlier_values(lax.optimization_barrier(jnp.sum(selectors[s - 1] * values, axis=1)), s)
        return result

    def operate(field):
        return backward(coherence * forward(field)) + DAMPING * field
    right = backward(coherence * sine_part)
    solution = jnp.zeros_like(right)
    remainder = right
    direction = right
    norm_now = lax.optimization_barrier(jnp.sum(remainder * remainder, axis=0))
    for step in range(ITERS):
        applied = operate(direction)
        step_size = norm_now / (lax.optimization_barrier(jnp.sum(direction * applied, axis=0)) + EPSILON)
        solution = solution + step_size * direction
        remainder = remainder - step_size * applied
        norm_next = lax.optimization_barrier(jnp.sum(remainder * remainder, axis=0))
        direction = remainder + norm_next / (norm_now + EPSILON) * direction
        norm_now = norm_next
    return solution

def reference(acquisitions, offsets):
    extended = jnp.pad(acquisitions, ((0, 0), (0, 0), (0, 0), (HC, HC)))
    date_ids = jnp.arange(DATES, dtype=jnp.int32)
    usable = (date_ids[:, None] + offsets < DATES).astype(jnp.float32)
    coherence, sine_part = pair_stats(extended, offsets, usable, DATES, True)
    by_rows = (jnp.moveaxis(coherence, 2, 0), jnp.moveaxis(sine_part, 2, 0))
    solved = lax.map(lambda pair: solve(pair[0], pair[1], offsets), by_rows)
    return (coherence, jnp.moveaxis(solved, 0, 1))
```

```python
import functools

import jax
import jax.numpy as jnp
from jax import lax
from jax.experimental import pallas as pl
from jax.experimental.pallas import tpu as pltpu
from jax.sharding import PartitionSpec as P

SPAN = 4
K = 3
HR = 2
HC = 7
ITERS = 6
DAMPING = 0.05
EPSILON = 1e-06

LANES = 128
ROWS = 32
GROUPS = ROWS // 8
FIELDS = 80
F32 = jnp.float32
BF16 = jnp.bfloat16


def lanes_of(shape):
    return lax.broadcasted_iota(jnp.int32, shape, len(shape) - 1)


def rows_of(shape):
    return lax.broadcasted_iota(jnp.int32, shape, len(shape) - 2)


def pack_kernel(acq_ref, packed_ref, rim_ref, corner_ref):
    dates = acq_ref.shape[1]
    lane = lanes_of((8, LANES))
    keep = (lane % 16) < 14
    for t in range(dates):
        total = jnp.zeros((8, LANES), F32)
        for f in range(2):
            for g in range(GROUPS):
                begin = 64 * f + 16 * g
                moved = pltpu.roll(acq_ref[f, t, 8 * g : 8 * g + 8, :], begin + HC, 1)
                total = jnp.where((lane >= begin) & (lane < begin + 14), moved, total)
        packed_ref[t] = total
        if t < SPAN:
            corner_ref[t] = total
    rim_ref[...] = acq_ref[:, :SPAN]


def thirds(values):
    high = values.astype(BF16)
    rest = values - high.astype(F32)
    middle = rest.astype(BF16)
    low = (rest - middle.astype(F32)).astype(BF16)
    return jnp.concatenate([high, middle, low], axis=1)


def row_window(parts):
    sub = rows_of((8, LANES))
    zero = jnp.zeros((8, LANES), F32)

    def up(x, n):
        rolled = [pltpu.roll(v, 8 - n, 0) for v in x] + [zero]
        return [jnp.where(sub < 8 - n, rolled[g], rolled[g + 1]) for g in range(GROUPS)]

    def down(x, n, above):
        rolled = [above] + [pltpu.roll(v, n, 0) for v in x]
        return [jnp.where(sub >= n, rolled[g + 1], rolled[g]) for g in range(GROUPS)]

    two = [a + b for a, b in zip(parts, up(parts, 1))]
    above = jnp.where(sub == 1, pltpu.roll(parts[0], 1, 0), 0.0)
    return [a + b + c for a, b, c in zip(parts, up(two, 1), down(two, 2, above))]


def pair_kernel(
    off_ref, acq_ref, rim_ref, left_ref, right_ref, corner_left_ref, corner_right_ref,
    out_ref, ext_ref, halo_ref, turned_ref, power_ref, right_side_ref, *, batch,
):
    dates = acq_ref.shape[1]
    total_dates = dates * lax.axis_size("date")
    first = lax.axis_index("date") * dates
    wide = dates + SPAN

    row = lax.broadcasted_iota(jnp.int32, (LANES, LANES), 0)
    col = lax.broadcasted_iota(jnp.int32, (LANES, LANES), 1)
    band = (jnp.abs(row - col) <= HC).astype(F32).astype(BF16)
    center_band = jnp.concatenate([band] * 3, axis=0)
    place = row % 16
    reach = ((place < HC) & (col <= place)) | (
        (place >= HC) & (place < 2 * HC) & (col >= LANES - 2 * HC + place)
    )
    halo_band = jnp.concatenate(
        [(reach & ((row % 64) // 16 == g)).astype(F32).astype(BF16) for g in range(GROUPS)], axis=1
    )
    halo_band = jnp.concatenate([halo_band] * 3, axis=0)

    ext_ref[:, :dates] = acq_ref[...]
    ext_ref[:, dates:] = rim_ref[...]
    lane = lanes_of((8, LANES))
    from_left = (lane % 16) < HC
    sign = jnp.where(lane < 64, -1.0, 1.0).astype(F32)
    for t in range(wide):
        if t < dates:
            halo = jnp.where(from_left, left_ref[t], right_ref[t])
        else:
            halo = jnp.where(from_left, corner_left_ref[t - dates], corner_right_ref[t - dates])
        halo_ref[t] = halo
        turned_ref[t] = pltpu.roll(halo, 64, 1) * sign
        right_side_ref[t] = jnp.zeros((ROWS, LANES), F32)

    def windows(products, halos):
        n = len(products)
        cols = jnp.dot(
            thirds(jnp.concatenate(products, axis=0)), center_band, preferred_element_type=F32
        )
        rims = jnp.dot(
            thirds(jnp.concatenate(halos, axis=0)), halo_band, preferred_element_type=F32
        )
        return [
            row_window(
                [
                    cols[ROWS * i + 8 * g : ROWS * i + 8 * g + 8]
                    + rims[8 * i : 8 * i + 8, LANES * g : LANES * (g + 1)]
                    for g in range(GROUPS)
                ]
            )
            for i in range(n)
        ]

    per = 11
    def power_step(step, carry):
        products, halos = [], []
        for i in range(per):
            t = step * per + i
            re, im = ext_ref[0, t], ext_ref[1, t]
            products.append(re * re + im * im)
            halos.append(halo_ref[t] * halo_ref[t])
        for i, parts in enumerate(windows(products, halos)):
            t = step * per + i
            for g in range(GROUPS):
                power_ref[t, 8 * g : 8 * g + 8, :] = parts[g]
        return carry

    lax.fori_loop(0, wide // per, power_step, 0)

    def pair_step(step, offsets_row):
        products, halos, seconds = [], [], []
        for i in range(batch):
            t = step * batch + i
            re, im, halo = ext_ref[0, t], ext_ref[1, t], halo_ref[t]
            for k in range(K):
                offset = off_ref[t, k]
                j = t + offset
                seconds.append((t, k, offset, j))
                re2, im2 = ext_ref[0, j], ext_ref[1, j]
                products.append(re * re2 + im * im2)
                products.append(im * re2 - re * im2)
                halos.append(halo * halo_ref[j])
                halos.append(halo * turned_ref[j])
        looked = windows(products, halos)
        for n, (t, k, offset, j) in enumerate(seconds):
            offsets_row = jnp.where(lane == K * t + k, offset.astype(F32), offsets_row)
            usable = jnp.where(first + j < total_dates, 1.0, 0.0).astype(F32)
            for g in range(GROUPS):
                rows = pl.ds(8 * g, 8)
                re, im = looked[2 * n][g], looked[2 * n + 1][g]
                scale = usable * lax.rsqrt(power_ref[t, rows, :] * power_ref[j, rows, :] + EPSILON)
                coherence = jnp.sqrt(re * re + im * im) * scale
                flow = coherence * (im * scale)
                out_ref[pl.ds(4 * g * 2 * FIELDS + K * t + k, 8, stride=FIELDS), :] = coherence
                right_side_ref[t, rows, :] = right_side_ref[t, rows, :] - flow
                right_side_ref[j, rows, :] = right_side_ref[j, rows, :] + flow
        return offsets_row

    offsets_row = lax.fori_loop(0, dates // batch, pair_step, jnp.zeros((8, LANES), F32))
    for g in range(GROUPS):
        base = 4 * g * 2 * FIELDS + K * dates
        for t in range(wide):
            out_ref[pl.ds(base + t, 8, stride=FIELDS), :] = right_side_ref[t, 8 * g : 8 * g + 8, :]
        for f in range(K * dates + wide, FIELDS):
            out_ref[pl.ds(4 * g * 2 * FIELDS + f, 8, stride=FIELDS), :] = offsets_row


def solve_kernel(recv_ref, coh_ref, disp_ref, weight_ref, p_ref, r_ref, x_ref, q_ref, *, dates):
    quarters = recv_ref.shape[0] // (8 * FIELDS)
    chunk = 2 * FIELDS
    sub = rows_of((8, LANES))
    zero = jnp.zeros((8, LANES), F32)

    def received(quarter, f):
        return recv_ref[pl.ds(quarter * 8 * FIELDS + f, 8, stride=FIELDS), :]

    for d in range(4 * quarters):
        for row in range(2):
            coh_ref[pl.ds(d * 2 * K * dates + row, K * dates, stride=2), :] = recv_ref[
                pl.ds(d * chunk + row * FIELDS, K * dates), :
            ]

    def one_block_later(get, quarter):
        near = pltpu.roll(get(quarter), 6, 0)
        far = pltpu.roll(get(quarter + 1), 6, 0) if quarter + 1 < quarters else zero
        return jnp.where(sub < 6, near, far)

    def one_block_earlier(get, quarter):
        near = pltpu.roll(get(quarter), 2, 0)
        far = pltpu.roll(get(quarter - 1), 2, 0) if quarter > 0 else zero
        return jnp.where(sub >= 2, near, far)

    def over_dates(v):
        v = v + pltpu.roll(v, 4, 0)
        return v + pltpu.roll(v, 2, 0)

    def refresh_ghosts():
        for quarter in range(quarters):
            for e in range(SPAN):
                p_ref[quarter, SPAN + dates + e] = one_block_later(
                    lambda n: p_ref[n, SPAN + e], quarter
                )
                p_ref[quarter, e] = one_block_earlier(lambda n: p_ref[n, dates + e], quarter)

    rr = zero
    for quarter in range(quarters):
        offsets = received(quarter, K * dates + dates + SPAN)
        for u in range(dates):
            values = [received(quarter, K * u + k) for k in range(K)]
            places = [
                jnp.broadcast_to(offsets[:, K * u + k : K * u + k + 1], (8, LANES)) for k in range(K)
            ]
            for s in range(1, SPAN + 1):
                weight = zero
                for k in range(K):
                    weight = jnp.where(places[k] == float(s), values[k], weight)
                weight_ref[s - 1, quarter, SPAN + u] = weight
            b = received(quarter, K * dates + u)
            if u < SPAN:
                b = b + one_block_earlier(lambda n: received(n, K * dates + dates + u), quarter)
            p_ref[quarter, SPAN + u] = b
            r_ref[quarter, u] = b
            x_ref[pl.ds((quarter * dates + u) * 8, 8), :] = zero
            rr = rr + b * b
    for quarter in range(quarters):
        for s in range(1, SPAN + 1):
            for e in range(SPAN - s, SPAN):
                weight_ref[s - 1, quarter, e] = one_block_earlier(
                    lambda n: weight_ref[s - 1, n, dates + e], quarter
                )
    rr = over_dates(rr)
    refresh_ghosts()

    def iteration(step, rr):
        pq = zero
        for quarter in range(quarters):
            flows = {}
            for e in range(dates + SPAN):
                here = p_ref[quarter, e]
                out = None
                for s in range(1, SPAN + 1):
                    if e >= SPAN - s:
                        flow = weight_ref[s - 1, quarter, e] * (p_ref[quarter, e + s] - here)
                        flows[s, e] = flow
                        if e >= SPAN:
                            term = flows.pop((s, e - s)) - flow
                            out = term if out is None else out + term
                if e >= SPAN:
                    out = out + DAMPING * here
                    q_ref[quarter, e - SPAN] = out
                    pq = pq + here * out
        a = rr / (over_dates(pq) + EPSILON)
        nn = zero
        for quarter in range(quarters):
            for u in range(dates):
                rows = pl.ds((quarter * dates + u) * 8, 8)
                x_ref[rows, :] = x_ref[rows, :] + a * p_ref[quarter, SPAN + u]
                rest = r_ref[quarter, u] - a * q_ref[quarter, u]
                r_ref[quarter, u] = rest
                nn = nn + rest * rest
        nn = over_dates(nn)
        ratio = nn / (rr + EPSILON)
        for quarter in range(quarters):
            for u in range(dates):
                p_ref[quarter, SPAN + u] = r_ref[quarter, u] + ratio * p_ref[quarter, SPAN + u]
        refresh_ghosts()
        return nn

    lax.fori_loop(0, ITERS, iteration, rr)
    for quarter in range(quarters):
        for j in range(4):
            for row in range(2):
                disp_ref[pl.ds((quarter * 4 + j) * 2 * dates + row, dates, stride=2), :] = x_ref[
                    pl.ds(quarter * dates * 8 + 2 * j + row, dates, stride=8), :
                ]


def vmem(count):
    return [pl.BlockSpec(memory_space=pltpu.VMEM)] * count


PARAMS = pltpu.CompilerParams(vmem_limit_bytes=48 * 1024 * 1024)


def local(acquisitions, offsets):
    dates = acquisitions.shape[1]
    blocks = lax.axis_size("date")
    tiles = lax.axis_size("pix")
    packed, rim, corner = pl.pallas_call(
        pack_kernel,
        out_shape=[
            jax.ShapeDtypeStruct((dates, 8, LANES), F32),
            jax.ShapeDtypeStruct((2, SPAN, ROWS, LANES), F32),
            jax.ShapeDtypeStruct((SPAN, 8, LANES), F32),
        ],
        in_specs=vmem(1),
        out_specs=vmem(3),
        compiler_params=PARAMS,
    )(acquisitions)

    def moved(x, dates_back, tiles_on):
        route = [
            (p * blocks + d, (p + tiles_on) * blocks + d - dates_back)
            for p in range(tiles)
            for d in range(blocks)
            if 0 <= p + tiles_on < tiles and d >= dates_back
        ]
        return lax.ppermute(x, ("pix", "date"), route)

    left = moved(packed, 0, 1)
    right = moved(packed, 0, -1)
    rim = moved(rim, 1, 0)
    corner_left = moved(corner, 1, 1)
    corner_right = moved(corner, 1, -1)

    wide = dates + SPAN
    messages = pl.pallas_call(
        functools.partial(pair_kernel, batch=3),
        out_shape=jax.ShapeDtypeStruct((blocks * 2 * FIELDS, LANES), F32),
        in_specs=[pl.BlockSpec(memory_space=pltpu.SMEM)] + vmem(6),
        out_specs=vmem(1)[0],
        scratch_shapes=[
            pltpu.VMEM((2, wide, ROWS, LANES), F32),
            pltpu.VMEM((wide, 8, LANES), F32),
            pltpu.VMEM((wide, 8, LANES), F32),
            pltpu.VMEM((wide, ROWS, LANES), F32),
            pltpu.VMEM((wide, ROWS, LANES), F32),
        ],
        compiler_params=PARAMS,
    )(offsets, acquisitions, rim, left, right, corner_left, corner_right)
    received = lax.all_to_all(messages, "date", split_axis=0, concat_axis=0, tiled=True)

    quarters = blocks // 4
    coherence, displacement = pl.pallas_call(
        functools.partial(solve_kernel, dates=dates),
        out_shape=[
            jax.ShapeDtypeStruct((blocks * dates * K * 2, LANES), F32),
            jax.ShapeDtypeStruct((blocks * dates * 2, LANES), F32),
        ],
        in_specs=vmem(1),
        out_specs=vmem(2),
        scratch_shapes=[
            pltpu.VMEM((SPAN, quarters, SPAN + dates, 8, LANES), F32),
            pltpu.VMEM((quarters, dates + 2 * SPAN, 8, LANES), F32),
            pltpu.VMEM((quarters, dates, 8, LANES), F32),
            pltpu.VMEM((quarters * dates * 8, LANES), F32),
            pltpu.VMEM((quarters, dates, 8, LANES), F32),
        ],
        compiler_params=PARAMS,
    )(received)
    return (
        coherence.reshape(blocks * dates, K, 2, LANES),
        displacement.reshape(blocks * dates, 2, LANES),
    )


def solution(mesh):
    placed = (P(None, "date", None, "pix"), P("date", None))
    return jax.shard_map(
        local,
        mesh=mesh,
        in_specs=placed,
        out_specs=(P(None, None, "date", "pix"), P(None, "date", "pix")),
        check_vma=False,
    )
```

```python
import functools

import jax
import jax.numpy as jnp
from jax import lax
from jax.experimental import pallas as pl
from jax.experimental.pallas import tpu as pltpu
from jax.sharding import PartitionSpec as P

SPAN = 4
K = 3
HR = 2
HC = 7
ITERS = 6
DAMPING = 0.05
EPSILON = 1e-06

LANES = 128
ROWS = 32
GROUPS = ROWS // 8
FIELDS = 80
F32 = jnp.float32
BF16 = jnp.bfloat16


def lanes_of(shape):
    return lax.broadcasted_iota(jnp.int32, shape, len(shape) - 1)


def rows_of(shape):
    return lax.broadcasted_iota(jnp.int32, shape, len(shape) - 2)


def pack_kernel(acq_ref, packed_ref, kept_ref, rim_ref):
    lane = lanes_of((8, LANES))
    for t in range(acq_ref.shape[1]):
        total = jnp.zeros((8, LANES), F32)
        for f in range(2):
            for g in range(GROUPS):
                begin = 64 * f + 16 * g
                here = acq_ref[f, t, 8 * g : 8 * g + 8, :]
                kept_ref[f, t, 8 * g : 8 * g + 8, :] = here
                if t < SPAN:
                    rim_ref[f, t, 8 * g : 8 * g + 8, :] = here
                moved = pltpu.roll(here, begin + HC, 1)
                total = jnp.where((lane >= begin) & (lane < begin + 2 * HC), moved, total)
        packed_ref[t] = total


def edges(left, right):
    tile, tiles = lax.axis_index("pix"), lax.axis_size("pix")
    lane = lanes_of(left.shape) % 16
    low = jnp.where(tile == 0, HC, 0)
    high = jnp.where(tile == tiles - 1, HC, 2 * HC)
    both = jnp.where(lane < HC, left, right)
    return jnp.where((lane >= low) & (lane < high), both, 0.0)


def thirds(values):
    high = values.astype(BF16)
    rest = values - high.astype(F32)
    middle = rest.astype(BF16)
    low = (rest - middle.astype(F32)).astype(BF16)
    return jnp.concatenate([high, middle, low], axis=1)


def row_window(parts):
    sub = rows_of((8, LANES))
    zero = jnp.zeros((8, LANES), F32)

    def up(x, n):
        rolled = [pltpu.roll(v, 8 - n, 0) for v in x] + [zero]
        return [jnp.where(sub < 8 - n, rolled[g], rolled[g + 1]) for g in range(GROUPS)]

    def down(x, n, above):
        rolled = [above] + [pltpu.roll(v, n, 0) for v in x]
        return [jnp.where(sub >= n, rolled[g + 1], rolled[g]) for g in range(GROUPS)]

    two = [a + b for a, b in zip(parts, up(parts, 1))]
    above = jnp.where(sub == 1, pltpu.roll(parts[0], 1, 0), 0.0)
    return [a + b + c for a, b, c in zip(parts, up(two, 1), down(two, 2, above))]


def center_band():
    row = lax.broadcasted_iota(jnp.int32, (LANES, LANES), 0)
    col = lax.broadcasted_iota(jnp.int32, (LANES, LANES), 1)
    band = (jnp.abs(row - col) <= HC).astype(F32).astype(BF16)
    return jnp.concatenate([band] * 3, axis=0)


def halo_band():
    row = lax.broadcasted_iota(jnp.int32, (LANES, LANES), 0)
    col = lax.broadcasted_iota(jnp.int32, (LANES, LANES), 1)
    place = row % 16
    reach = ((place < HC) & (col <= place)) | (
        (place >= HC) & (place < 2 * HC) & (col >= LANES - 2 * HC + place)
    )
    band = jnp.concatenate(
        [(reach & ((row % 64) // 16 == g)).astype(F32).astype(BF16) for g in range(GROUPS)], axis=1
    )
    return jnp.concatenate([band] * 3, axis=0)


def banded(fields, band):
    return jnp.dot(thirds(jnp.concatenate(fields, axis=0)), band, preferred_element_type=F32)


def products(first, second):
    (re, im), (re2, im2) = first, second
    return [re * re2 + im * im2, im * re2 - re * im2]


def turn(halo):
    sign = jnp.where(lanes_of((8, LANES)) < 64, -1.0, 1.0).astype(F32)
    return pltpu.roll(halo, 64, 1) * sign


def windows(column_sums, halos, band):
    rims = banded(halos, band)
    return [
        row_window(
            [
                column_sums(i, g) + rims[8 * i : 8 * i + 8, LANES * g : LANES * (g + 1)]
                for g in range(GROUPS)
            ]
        )
        for i in range(len(halos))
    ]


def center_kernel(off_in, acq_ref, sums_ref, off_ref, sem, *, near, batch):
    dates = acq_ref.shape[1]
    copy = pltpu.make_async_copy(off_in, off_ref, sem)
    copy.start()
    band = center_band()

    def power_step(step, carry):
        fields = []
        for i in range(dates // 2):
            re, im = acq_ref[0, step * (dates // 2) + i], acq_ref[1, step * (dates // 2) + i]
            fields.append(re * re + im * im)
        cols = banded(fields, band)
        for i in range(dates // 2):
            sums_ref[2 * K * near + step * (dates // 2) + i] = cols[ROWS * i : ROWS * (i + 1)]
        return carry

    lax.fori_loop(0, 2, power_step, 0)

    copy.wait()

    def pair_step(step, carry):
        fields = []
        for i in range(batch):
            t = step * batch + i
            first = acq_ref[0, t], acq_ref[1, t]
            for k in range(K):
                j = t + off_ref[k, t]
                fields += products(first, (acq_ref[0, j], acq_ref[1, j]))
        cols = banded(fields, band)
        for i in range(2 * K * batch):
            sums_ref[2 * K * batch * step + i] = cols[ROWS * i : ROWS * (i + 1)]
        return carry

    lax.fori_loop(0, near // batch, pair_step, 0)


def finish_pair(looked, t, k, offset, usable, power_ref, out_ref, right_side_ref):
    j = t + offset
    for g in range(GROUPS):
        rows = pl.ds(8 * g, 8)
        re, im = looked[0][g], looked[1][g]
        scale = lax.rsqrt(power_ref[t, rows, :] * power_ref[j, rows, :] + EPSILON)
        if usable is not None:
            scale = usable * scale
        coherence = jnp.sqrt(re * re + im * im) * scale
        flow = coherence * (im * scale)
        out_ref[pl.ds(8 * g * FIELDS + K * t + k, 8, stride=FIELDS), :] = coherence
        right_side_ref[t, rows, :] = right_side_ref[t, rows, :] - flow
        right_side_ref[j, rows, :] = right_side_ref[j, rows, :] + flow


def near_kernel(
    off_in, acq_ref, rim_ref, left_ref, right_ref, sums_ref,
    out_ref, halo_ref, power_ref, right_side_ref, far_sums_ref, turned_ref, next_ref, off_ref, sem, *, near, batch,
):
    dates = acq_ref.shape[1]
    copy = pltpu.make_async_copy(off_in, off_ref, sem)
    copy.start()
    band = halo_band()
    for t in range(dates + SPAN):
        right_side_ref[t] = jnp.zeros((ROWS, LANES), F32)
    for t in range(dates):
        halo = edges(left_ref[t], right_ref[t])
        halo_ref[t] = halo
        turned_ref[t] = turn(halo)

    half = dates // 2

    def power_step(step, carry):
        halos = [halo_ref[step * half + i] * halo_ref[step * half + i] for i in range(half)]

        def column_sums(i, g):
            return sums_ref[2 * K * near + step * half + i, 8 * g : 8 * g + 8, :]

        for i, parts in enumerate(windows(column_sums, halos, band)):
            for g in range(GROUPS):
                power_ref[step * half + i, 8 * g : 8 * g + 8, :] = parts[g]
        return carry

    lax.fori_loop(0, 2, power_step, 0)

    copy.wait()

    def pair_step(step, carry):
        halos, pairs = [], []
        for i in range(batch):
            t = step * batch + i
            halo = halo_ref[t]
            for k in range(K):
                offset = off_ref[k, t]
                pairs.append((t, k, offset))
                halos += [halo * halo_ref[t + offset], halo * turned_ref[t + offset]]

        def column_sums(i, g):
            return sums_ref[2 * K * batch * step + i, 8 * g : 8 * g + 8, :]

        looked = windows(column_sums, halos, band)
        for n, (t, k, offset) in enumerate(pairs):
            finish_pair(
                looked[2 * n : 2 * n + 2], t, k, offset, None, power_ref, out_ref, right_side_ref
            )
        return carry

    lax.fori_loop(0, near // batch, pair_step, 0)

    for t in range(near):
        for g in range(GROUPS):
            out_ref[pl.ds(8 * g * FIELDS + K * dates + t, 8, stride=FIELDS), :] = right_side_ref[
                t, 8 * g : 8 * g + 8, :
            ]

    fields = []
    last = lax.axis_index("date") == lax.axis_size("date") - 1
    for t in range(SPAN):
        for f in range(2):
            next_ref[f, t] = jnp.where(last, 0.0, rim_ref[f, t])
        re, im = next_ref[0, t], next_ref[1, t]
        fields.append(re * re + im * im)
    for t in range(near, dates):
        first = acq_ref[0, t], acq_ref[1, t]
        for k in range(K):
            j = t + off_ref[k, t]
            inside = j < dates
            j_in, j_out = jnp.minimum(j, dates - 1), jnp.maximum(j - dates, 0)
            second = [jnp.where(inside, acq_ref[f, j_in], next_ref[f, j_out]) for f in range(2)]
            fields += products(first, second)
    cols = banded(fields, center_band())
    for i in range(len(fields)):
        far_sums_ref[i] = cols[ROWS * i : ROWS * (i + 1)]


def far_kernel(
    off_in, message_ref, near_halo_ref, corner_ref, near_power_ref, near_right_ref, sums_ref,
    out_ref, halo_ref, turned_ref, power_ref, right_side_ref, off_ref, sem, *, near,
):
    del message_ref
    copy = pltpu.make_async_copy(off_in, off_ref, sem)
    copy.start()
    dates = near_halo_ref.shape[0]
    total_dates = dates * lax.axis_size("date")
    first = lax.axis_index("date") * dates
    band = halo_band()
    for t in range(near, dates + SPAN):
        halo = near_halo_ref[t] if t < dates else corner_ref[t - dates]
        halo_ref[t] = halo
        turned_ref[t] = turn(halo)
        right_side_ref[t] = near_right_ref[t]
        if t < dates:
            power_ref[t] = near_power_ref[t]

    halos = [halo_ref[dates + t] * halo_ref[dates + t] for t in range(SPAN)]
    powers = windows(lambda i, g: sums_ref[i, 8 * g : 8 * g + 8, :], halos, band)
    for t in range(SPAN):
        for g in range(GROUPS):
            power_ref[dates + t, 8 * g : 8 * g + 8, :] = powers[t][g]
    copy.wait()
    pairs, halos = [], []
    for t in range(near, dates):
        for k in range(K):
            offset = off_ref[k, t]
            pairs.append((t, k, offset))
            halos += [halo_ref[t] * halo_ref[t + offset], halo_ref[t] * turned_ref[t + offset]]
    looked = windows(lambda i, g: sums_ref[SPAN + i, 8 * g : 8 * g + 8, :], halos, band)
    for n, (t, k, offset) in enumerate(pairs):
        usable = jnp.where(first + t + offset < total_dates, 1.0, 0.0).astype(F32)
        finish_pair(
            looked[2 * n : 2 * n + 2], t, k, offset, usable, power_ref, out_ref, right_side_ref
        )
    lane = lanes_of((8, LANES))
    offsets_row = jnp.zeros((8, LANES), F32)
    for t in range(dates):
        for k in range(K):
            offsets_row = jnp.where(lane == K * t + k, off_ref[k, t].astype(F32), offsets_row)
    for g in range(GROUPS):
        base = 8 * g * FIELDS + K * dates
        for t in range(near, dates + SPAN):
            out_ref[pl.ds(base + t, 8, stride=FIELDS), :] = right_side_ref[t, 8 * g : 8 * g + 8, :]
        for f in range(dates + SPAN, FIELDS - K * dates):
            out_ref[pl.ds(base + f, 8, stride=FIELDS), :] = offsets_row


def solve_kernel(recv_ref, coh_ref, disp_ref, weight_ref, p_ref, r_ref, x_ref, q_ref, *, dates):
    quarters = recv_ref.shape[0] // (8 * FIELDS)
    chunk = 2 * FIELDS
    sub = rows_of((8, LANES))
    zero = jnp.zeros((8, LANES), F32)

    def received(quarter, f):
        return recv_ref[pl.ds(quarter * 8 * FIELDS + f, 8, stride=FIELDS), :]

    for d in range(4 * quarters):
        for row in range(2):
            coh_ref[pl.ds(d * 2 * K * dates + row, K * dates, stride=2), :] = recv_ref[
                pl.ds(d * chunk + row * FIELDS, K * dates), :
            ]

    def one_block_later(get, quarter):
        near = pltpu.roll(get(quarter), 6, 0)
        far = pltpu.roll(get(quarter + 1), 6, 0) if quarter + 1 < quarters else zero
        return jnp.where(sub < 6, near, far)

    def one_block_earlier(get, quarter):
        near = pltpu.roll(get(quarter), 2, 0)
        far = pltpu.roll(get(quarter - 1), 2, 0) if quarter > 0 else zero
        return jnp.where(sub >= 2, near, far)

    def over_dates(v):
        v = v + pltpu.roll(v, 4, 0)
        return v + pltpu.roll(v, 2, 0)

    def refresh_ghosts():
        for quarter in range(quarters):
            for e in range(SPAN):
                p_ref[quarter, SPAN + dates + e] = one_block_later(
                    lambda n: p_ref[n, SPAN + e], quarter
                )
                p_ref[quarter, e] = one_block_earlier(lambda n: p_ref[n, dates + e], quarter)

    rr = zero
    for quarter in range(quarters):
        offsets = received(quarter, K * dates + dates + SPAN)
        for u in range(dates):
            values = [received(quarter, K * u + k) for k in range(K)]
            places = [
                jnp.broadcast_to(offsets[:, K * u + k : K * u + k + 1], (8, LANES)) for k in range(K)
            ]
            for s in range(1, SPAN + 1):
                weight = zero
                for k in range(K):
                    weight = jnp.where(places[k] == float(s), values[k], weight)
                weight_ref[s - 1, quarter, SPAN + u] = weight
            b = received(quarter, K * dates + u)
            if u < SPAN:
                b = b + one_block_earlier(lambda n: received(n, K * dates + dates + u), quarter)
            p_ref[quarter, SPAN + u] = b
            r_ref[quarter, u] = b
            x_ref[pl.ds((quarter * dates + u) * 8, 8), :] = zero
            rr = rr + b * b
    for quarter in range(quarters):
        for s in range(1, SPAN + 1):
            for e in range(SPAN - s, SPAN):
                weight_ref[s - 1, quarter, e] = one_block_earlier(
                    lambda n: weight_ref[s - 1, n, dates + e], quarter
                )
    rr = over_dates(rr)
    refresh_ghosts()

    def iteration(step, rr):
        pq = zero
        for quarter in range(quarters):
            flows = {}
            for e in range(dates + SPAN):
                here = p_ref[quarter, e]
                out = None
                for s in range(1, SPAN + 1):
                    if e >= SPAN - s:
                        flow = weight_ref[s - 1, quarter, e] * (p_ref[quarter, e + s] - here)
                        flows[s, e] = flow
                        if e >= SPAN:
                            term = flows.pop((s, e - s)) - flow
                            out = term if out is None else out + term
                if e >= SPAN:
                    out = out + DAMPING * here
                    q_ref[quarter, e - SPAN] = out
                    pq = pq + here * out
        a = rr / (over_dates(pq) + EPSILON)
        nn = zero
        for quarter in range(quarters):
            for u in range(dates):
                rows = pl.ds((quarter * dates + u) * 8, 8)
                x_ref[rows, :] = x_ref[rows, :] + a * p_ref[quarter, SPAN + u]
                rest = r_ref[quarter, u] - a * q_ref[quarter, u]
                r_ref[quarter, u] = rest
                nn = nn + rest * rest
        nn = over_dates(nn)
        ratio = nn / (rr + EPSILON)
        for quarter in range(quarters):
            for u in range(dates):
                p_ref[quarter, SPAN + u] = r_ref[quarter, u] + ratio * p_ref[quarter, SPAN + u]
        refresh_ghosts()
        return nn

    lax.fori_loop(0, ITERS, iteration, rr)
    for quarter in range(quarters):
        for j in range(4):
            for row in range(2):
                disp_ref[pl.ds((quarter * 4 + j) * 2 * dates + row, dates, stride=2), :] = x_ref[
                    pl.ds(quarter * dates * 8 + 2 * j + row, dates, stride=8), :
                ]


def vmem(count):
    return [pl.BlockSpec(memory_space=pltpu.VMEM)] * count


PARAMS = pltpu.CompilerParams(vmem_limit_bytes=48 * 1024 * 1024)


def shape(*sizes):
    return jax.ShapeDtypeStruct(sizes, F32)


def local(acquisitions, offsets):
    dates = acquisitions.shape[1]
    blocks = lax.axis_size("date")
    tiles = lax.axis_size("pix")
    near, wide = dates - SPAN, dates + SPAN
    anywhere = [pl.BlockSpec(memory_space=pl.ANY)]
    table = [pltpu.SMEM((K, dates), jnp.int32), pltpu.SemaphoreType.DMA]
    offsets = offsets.T
    packed, kept, rim = pl.pallas_call(
        pack_kernel,
        out_shape=[
            shape(dates, 8, LANES), shape(2, dates, ROWS, LANES), shape(2, SPAN, ROWS, LANES)
        ],
        in_specs=vmem(1),
        out_specs=vmem(3),
        compiler_params=PARAMS,
    )(acquisitions)

    up = [(p, (p + 1) % tiles) for p in range(tiles)]
    left = lax.ppermute(packed, "pix", up)
    right = lax.ppermute(packed, "pix", [(j, i) for i, j in up])
    back = [((d + 1) % blocks, d) for d in range(blocks)]
    rim = lax.ppermute(rim, "date", back)

    sums = pl.pallas_call(
        functools.partial(center_kernel, near=near, batch=7),
        out_shape=shape(2 * K * near + dates, ROWS, LANES),
        in_specs=anywhere + vmem(1),
        out_specs=vmem(1)[0],
        scratch_shapes=table,
        compiler_params=PARAMS,
    )(offsets, kept)

    def corner_kernel(left_ref, right_ref, sums_ref, out_ref):
        del sums_ref
        for t in range(SPAN):
            out_ref[t] = edges(left_ref[t], right_ref[t])

    corner = pl.pallas_call(
        corner_kernel,
        out_shape=shape(SPAN, 8, LANES),
        in_specs=vmem(2) + anywhere,
        out_specs=vmem(1)[0],
        compiler_params=PARAMS,
    )(left, right, sums)
    corner = lax.ppermute(corner, "date", back)

    messages, halo, power, right_side, far_sums = pl.pallas_call(
        functools.partial(near_kernel, near=near, batch=7),
        out_shape=[
            shape(blocks * 2 * FIELDS, LANES),
            shape(dates, 8, LANES),
            shape(dates, ROWS, LANES),
            shape(wide, ROWS, LANES),
            shape(SPAN + 2 * K * SPAN, ROWS, LANES),
        ],
        in_specs=anywhere + vmem(5),
        out_specs=vmem(5),
        scratch_shapes=[
            pltpu.VMEM((dates, 8, LANES), F32),
            pltpu.VMEM((2, SPAN, ROWS, LANES), F32),
            *table,
        ],
        compiler_params=PARAMS,
    )(offsets, kept, rim, left, right, sums)

    messages = pl.pallas_call(
        functools.partial(far_kernel, near=near),
        out_shape=shape(blocks * 2 * FIELDS, LANES),
        in_specs=anywhere + vmem(6),
        out_specs=vmem(1)[0],
        input_output_aliases={1: 0},
        scratch_shapes=[
            pltpu.VMEM((wide, 8, LANES), F32),
            pltpu.VMEM((wide, 8, LANES), F32),
            pltpu.VMEM((wide, ROWS, LANES), F32),
            pltpu.VMEM((wide, ROWS, LANES), F32),
            *table,
        ],
        compiler_params=PARAMS,
    )(offsets, messages, halo, corner, power, right_side, far_sums)
    received = lax.all_to_all(messages, "date", split_axis=0, concat_axis=0, tiled=True)

    quarters = blocks // 4
    coherence, displacement = pl.pallas_call(
        functools.partial(solve_kernel, dates=dates),
        out_shape=[
            jax.ShapeDtypeStruct((blocks * dates * K * 2, LANES), F32),
            jax.ShapeDtypeStruct((blocks * dates * 2, LANES), F32),
        ],
        in_specs=vmem(1),
        out_specs=vmem(2),
        scratch_shapes=[
            pltpu.VMEM((SPAN, quarters, SPAN + dates, 8, LANES), F32),
            pltpu.VMEM((quarters, dates + 2 * SPAN, 8, LANES), F32),
            pltpu.VMEM((quarters, dates, 8, LANES), F32),
            pltpu.VMEM((quarters * dates * 8, LANES), F32),
            pltpu.VMEM((quarters, dates, 8, LANES), F32),
        ],
        compiler_params=PARAMS,
    )(received)
    return (
        coherence.reshape(blocks * dates, K, 2, LANES),
        displacement.reshape(blocks * dates, 2, LANES),
    )


def solution(mesh):
    placed = (P(None, "date", None, "pix"), P("date", None))
    return jax.shard_map(
        local,
        mesh=mesh,
        in_specs=placed,
        out_specs=(P(None, None, "date", "pix"), P(None, "date", "pix")),
        check_vma=False,
    )
```

```python
import functools

import jax
import jax.numpy as jnp
from jax import lax
from jax.experimental import pallas as pl
from jax.experimental.pallas import tpu as pltpu
from jax.sharding import PartitionSpec as P

SPAN = 4
K = 3
HR = 2
HC = 7
ITERS = 6
DAMPING = 0.05
EPSILON = 1e-06

LANES = 128
ROWS = 32
GROUPS = ROWS // 8
FIELDS = 76
F32 = jnp.float32
BF16 = jnp.bfloat16


def lanes_of(shape):
    return lax.broadcasted_iota(jnp.int32, shape, len(shape) - 1)


def rows_of(shape):
    return lax.broadcasted_iota(jnp.int32, shape, len(shape) - 2)


def pack_kernel(acq_ref, packed_ref, kept_ref, rim_ref):
    lane = lanes_of((8, LANES))
    for t in range(acq_ref.shape[1]):
        total = jnp.zeros((8, LANES), F32)
        for f in range(2):
            for g in range(GROUPS):
                begin = 64 * f + 16 * g
                here = acq_ref[f, t, 8 * g : 8 * g + 8, :]
                kept_ref[f, t, 8 * g : 8 * g + 8, :] = here
                if t < SPAN:
                    rim_ref[f, t, 8 * g : 8 * g + 8, :] = here
                moved = pltpu.roll(here, begin + HC, 1)
                total = jnp.where((lane >= begin) & (lane < begin + 2 * HC), moved, total)
        packed_ref[t] = total


def edges(left, right):
    tile, tiles = lax.axis_index("pix"), lax.axis_size("pix")
    lane = lanes_of(left.shape) % 16
    low = jnp.where(tile == 0, HC, 0)
    high = jnp.where(tile == tiles - 1, HC, 2 * HC)
    both = jnp.where(lane < HC, left, right)
    return jnp.where((lane >= low) & (lane < high), both, 0.0)


def halves(values):
    high = values.astype(BF16)
    return jnp.concatenate([high, (values - high.astype(F32)).astype(BF16)], axis=1)


def row_window(parts):
    sub = rows_of((8, LANES))
    zero = jnp.zeros((8, LANES), F32)

    def up(x, n, below):
        x = x + [below]
        return [pltpu.roll(jnp.where(sub >= n, x[g], x[g + 1]), 8 - n, 0) for g in range(GROUPS)]

    def down(x, n, above):
        x = [above] + x
        return [pltpu.roll(jnp.where(sub < 8 - n, x[g + 1], x[g]), n, 0) for g in range(GROUPS)]

    two = [a + b for a, b in zip(parts, up(parts, 1, zero))]
    above = jnp.where(sub == 7, pltpu.roll(parts[0], 7, 0), 0.0)
    return [a + b + c for a, b, c in zip(parts, up(two, 1, zero), down(two, 2, above))]


def packed_window(x):
    sub, place = rows_of((8, LANES)), lanes_of((8, LANES)) % 64
    below = jnp.where(place < 48, pltpu.roll(x, LANES - 16, 1), 0.0)
    above = jnp.where(place >= 16, pltpu.roll(x, 16, 1), 0.0)
    total = x
    for n in range(1, HR + 1):
        total = total + pltpu.roll(jnp.where(sub >= n, x, below), 8 - n, 0)
        total = total + pltpu.roll(jnp.where(sub < 8 - n, x, above), n, 0)
    return total


def center_band():
    row = lax.broadcasted_iota(jnp.int32, (LANES, LANES), 0)
    col = lax.broadcasted_iota(jnp.int32, (LANES, LANES), 1)
    band = (jnp.abs(row - col) <= HC).astype(F32).astype(BF16)
    return jnp.concatenate([band] * 2, axis=0)


def halo_band():
    row = lax.broadcasted_iota(jnp.int32, (LANES, LANES), 0)
    col = lax.broadcasted_iota(jnp.int32, (LANES, LANES), 1)
    place = row % 16
    reach = ((place < HC) & (col <= place)) | (
        (place >= HC) & (place < 2 * HC) & (col >= LANES - 2 * HC + place)
    )
    band = jnp.concatenate(
        [(reach & ((row % 64) // 16 == g)).astype(F32).astype(BF16) for g in range(GROUPS)], axis=1
    )
    return jnp.concatenate([band] * 2, axis=0)


def banded(fields, band):
    return jnp.dot(halves(jnp.concatenate(fields, axis=0)), band, preferred_element_type=F32)


def products(first, second):
    (re, im), (re2, im2) = first, second
    return [re * re2 + im * im2, im * re2 - re * im2]


def turn(halo):
    sign = jnp.where(lanes_of((8, LANES)) < 64, -1.0, 1.0).astype(F32)
    return pltpu.roll(halo, 64, 1) * sign


def center_windows(fields, band, out_ref, at):
    cols = banded(fields, band)
    for i in range(len(fields)):
        parts = [cols[ROWS * i + 8 * g : ROWS * i + 8 * g + 8] for g in range(GROUPS)]
        for g, part in enumerate(row_window(parts)):
            out_ref[at + i, 8 * g : 8 * g + 8, :] = part


def windows(center_ref, at, halos, band):
    rims = banded([packed_window(halo) for halo in halos], band)
    return [
        [
            center_ref[at + i, 8 * g : 8 * g + 8, :]
            + rims[8 * i : 8 * i + 8, LANES * g : LANES * (g + 1)]
            for g in range(GROUPS)
        ]
        for i in range(len(halos))
    ]


def chosen(offset, candidates):
    result = candidates[-1]
    for s in range(len(candidates) - 1, 0, -1):
        result = jnp.where(offset == float(s), candidates[s - 1], result)
    return result


def pair_fields(value, table_ref, dates):
    fields = []
    for t in dates:
        first = [[value(f, t, g) for f in range(2)] for g in range(GROUPS)]
        for k in range(K):
            offset = table_ref[K * t + k]
            pairs = [
                products(
                    first[g],
                    [
                        chosen(offset, [value(f, t + s, g) for s in range(1, SPAN + 1)])
                        for f in range(2)
                    ],
                )
                for g in range(GROUPS)
            ]
            fields += [jnp.concatenate([pair[c] for pair in pairs], axis=0) for c in range(2)]
    return fields


def power_fields(value, dates):
    fields = []
    for t in dates:
        parts = [[value(f, t, g) for f in range(2)] for g in range(GROUPS)]
        fields.append(jnp.concatenate([re * re + im * im for re, im in parts], axis=0))
    return fields


def center_kernel(off_ref, acq_ref, sums_ref, table_ref, *, near, batch):
    dates = acq_ref.shape[1]
    band = center_band()
    lane = lanes_of((8, LANES))
    row = jnp.zeros((8, LANES), F32)
    offsets = off_ref[...].astype(F32)
    for t in range(dates):
        for k in range(K):
            offset = jnp.broadcast_to(offsets[k : k + 1, t : t + 1], (8, LANES))
            table_ref[K * t + k] = offset
            row = jnp.where(lane == K * t + k, offset, row)
    table_ref[K * dates] = row

    def value(f, t, g):
        return acq_ref[f, t, 8 * g : 8 * g + 8, :]

    for begin in range(0, dates, dates // 2):
        fields = power_fields(value, range(begin, begin + dates // 2))
        center_windows(fields, band, sums_ref, 2 * K * near + begin)
    for begin in range(0, near, batch):
        fields = pair_fields(value, table_ref, range(begin, begin + batch))
        center_windows(fields, band, sums_ref, 2 * K * begin)


def far_center_kernel(table_ref, acq_ref, rim_ref, sums_ref, *, near):
    dates = acq_ref.shape[1]
    last = lax.axis_index("date") == lax.axis_size("date") - 1

    def value(f, t, g):
        rows = pl.ds(8 * g, 8)
        if t < dates:
            return acq_ref[f, t, rows, :]
        return jnp.where(last, 0.0, rim_ref[f, t - dates, rows, :])

    fields = power_fields(value, range(dates, dates + SPAN))
    fields += pair_fields(value, table_ref, range(near, dates))
    center_windows(fields, center_band(), sums_ref, 0)


def halo_pairs(table_ref, halo, turned, dates):
    fields = []
    for t in dates:
        for k in range(K):
            for field in (halo, turned):
                second = chosen(table_ref[K * t + k], [field(t + s) for s in range(1, SPAN + 1)])
                fields.append(halo(t) * second)
    return fields


def finish(looked, t, table_ref, power, limit, out_ref, add):
    offsets = [table_ref[K * t + k] for k in range(K)]
    for g in range(GROUPS):
        flows = []
        for k in range(K):
            re, im = looked[2 * k][g], looked[2 * k + 1][g]
            second = chosen(offsets[k], [power(t + s, g) for s in range(1, SPAN + 1)])
            scale = lax.rsqrt(power(t, g) * second + EPSILON)
            if limit is not None:
                scale = jnp.where(offsets[k] < limit, scale, 0.0)
            coherence = jnp.sqrt(re * re + im * im) * scale
            out_ref[pl.ds(8 * g * FIELDS + K * t + k, 8, stride=FIELDS), :] = coherence
            flows.append(coherence * (im * scale))
        total = flows[0]
        for flow in flows[1:]:
            total = total + flow
        add(t, g, -total)
        for s in range(1, SPAN + 1):
            share = jnp.zeros((8, LANES), F32)
            for offset, flow in zip(offsets, flows):
                share = jnp.where(offset == float(s), flow, share)
            add(t + s, g, share)


def near_kernel(
    table_ref, left_ref, right_ref, sums_ref,
    out_ref, halo_ref, power_ref, partial_ref, turned_ref, right_side_ref, *, near, batch,
):
    dates = left_ref.shape[0]
    band = halo_band()
    for t in range(dates):
        halo = edges(left_ref[t], right_ref[t])
        halo_ref[t] = halo
        turned_ref[t] = turn(halo)
        right_side_ref[t] = jnp.zeros((ROWS, LANES), F32)
    halos = [halo_ref[t] * halo_ref[t] for t in range(dates)]
    for t, parts in enumerate(windows(sums_ref, 2 * K * near, halos, band)):
        for g in range(GROUPS):
            power_ref[t, 8 * g : 8 * g + 8, :] = parts[g]

    def power(t, g):
        return power_ref[t, 8 * g : 8 * g + 8, :]

    def add(t, g, x):
        rows = pl.ds(8 * g, 8)
        right_side_ref[t, rows, :] = right_side_ref[t, rows, :] + x

    for begin in range(0, near, batch):
        group = range(begin, begin + batch)
        halos = halo_pairs(table_ref, lambda t: halo_ref[t], lambda t: turned_ref[t], group)
        looked = windows(sums_ref, 2 * K * begin, halos, band)
        for i, t in enumerate(group):
            finish(looked[2 * K * i : 2 * K * (i + 1)], t, table_ref, power, None, out_ref, add)
    for t in range(near):
        for g in range(GROUPS):
            out_ref[pl.ds(8 * g * FIELDS + K * dates + t, 8, stride=FIELDS), :] = right_side_ref[
                t, 8 * g : 8 * g + 8, :
            ]
    partial_ref[...] = right_side_ref[near:]


def far_kernel(
    table_ref, message_ref, near_halo_ref, corner_ref, near_power_ref, partial_ref, sums_ref,
    out_ref, right_side_ref, *, near,
):
    del message_ref
    dates = near_halo_ref.shape[0]
    total_dates = dates * lax.axis_size("date")
    first = lax.axis_index("date") * dates
    halo = {t: near_halo_ref[t] for t in range(near, dates)}
    for t in range(SPAN):
        halo[dates + t] = corner_ref[t]
        right_side_ref[t] = partial_ref[t]
        right_side_ref[SPAN + t] = jnp.zeros((ROWS, LANES), F32)
    turned = {t: turn(halo[t]) for t in halo}
    halos = [halo[t] * halo[t] for t in range(dates, dates + SPAN)]
    halos += halo_pairs(table_ref, lambda t: halo[t], lambda t: turned[t], range(near, dates))
    sums = windows(sums_ref, 0, halos, halo_band())

    def power(t, g):
        return sums[t - dates][g] if t >= dates else near_power_ref[t, 8 * g : 8 * g + 8, :]

    def add(t, g, x):
        rows = pl.ds(8 * g, 8)
        right_side_ref[t - near, rows, :] = right_side_ref[t - near, rows, :] + x

    for t in range(near, dates):
        n = SPAN + 2 * K * (t - near)
        limit = (total_dates - first - t).astype(F32)
        finish(sums[n : n + 2 * K], t, table_ref, power, limit, out_ref, add)
    for g in range(GROUPS):
        base = 8 * g * FIELDS + K * dates
        for t in range(near, dates + SPAN - 1):
            out_ref[pl.ds(base + t, 8, stride=FIELDS), :] = right_side_ref[
                t - near, 8 * g : 8 * g + 8, :
            ]
        out_ref[pl.ds(base + dates + SPAN - 1, 8, stride=FIELDS), :] = table_ref[K * dates]


def solve_kernel(
    recv_ref, coh_out, disp_ref, coh_ref, weight_ref, p_ref, r_ref, x_ref, q_ref, sem, *, dates
):
    quarters = recv_ref.shape[0] // (8 * FIELDS)
    chunk = 2 * FIELDS
    sub = rows_of((8, LANES))
    zero = jnp.zeros((8, LANES), F32)

    def received(quarter, f):
        return recv_ref[pl.ds(quarter * 8 * FIELDS + f, 8, stride=FIELDS), :]

    for d in range(4 * quarters):
        for row in range(2):
            coh_ref[pl.ds(d * 2 * K * dates + row, K * dates, stride=2), :] = recv_ref[
                pl.ds(d * chunk + row * FIELDS, K * dates), :
            ]
    copy = pltpu.make_async_copy(coh_ref, coh_out, sem)
    copy.start()

    def one_block_later(get, quarter):
        near = pltpu.roll(get(quarter), 6, 0)
        far = pltpu.roll(get(quarter + 1), 6, 0) if quarter + 1 < quarters else zero
        return jnp.where(sub < 6, near, far)

    def one_block_earlier(get, quarter):
        near = pltpu.roll(get(quarter), 2, 0)
        far = pltpu.roll(get(quarter - 1), 2, 0) if quarter > 0 else zero
        return jnp.where(sub >= 2, near, far)

    def over_dates(v):
        v = v + pltpu.roll(v, 4, 0)
        return v + pltpu.roll(v, 2, 0)

    def refresh_ghosts():
        for quarter in range(quarters):
            for e in range(SPAN):
                p_ref[quarter, SPAN + dates + e] = one_block_later(
                    lambda n: p_ref[n, SPAN + e], quarter
                )
                p_ref[quarter, e] = one_block_earlier(lambda n: p_ref[n, dates + e], quarter)

    rr = zero
    rims = []
    for quarter in range(quarters):
        rim = [received(quarter, K * dates + dates + e) for e in range(SPAN - 1)]
        rest = rim[0] + rim[1] + rim[2]
        for u in range(dates):
            rest = rest + received(quarter, K * dates + u)
        rims.append(rim + [-rest])
    for quarter in range(quarters):
        offsets = received(quarter, K * dates + dates + SPAN - 1)
        for u in range(dates):
            values = [received(quarter, K * u + k) for k in range(K)]
            places = [
                jnp.broadcast_to(offsets[:, K * u + k : K * u + k + 1], (8, LANES)) for k in range(K)
            ]
            for s in range(1, SPAN + 1):
                weight = zero
                for k in range(K):
                    weight = jnp.where(places[k] == float(s), values[k], weight)
                weight_ref[s - 1, quarter, SPAN + u] = weight
            b = received(quarter, K * dates + u)
            if u < SPAN:
                b = b + one_block_earlier(lambda n: rims[n][u], quarter)
            p_ref[quarter, SPAN + u] = b
            r_ref[quarter, u] = b
            x_ref[pl.ds((quarter * dates + u) * 8, 8), :] = zero
            rr = rr + b * b
    for quarter in range(quarters):
        for s in range(1, SPAN + 1):
            for e in range(SPAN - s, SPAN):
                weight_ref[s - 1, quarter, e] = one_block_earlier(
                    lambda n: weight_ref[s - 1, n, dates + e], quarter
                )
    rr = over_dates(rr)
    refresh_ghosts()

    def iteration(step, rr):
        pq = zero
        for quarter in range(quarters):
            flows = {}
            for e in range(dates + SPAN):
                here = p_ref[quarter, e]
                out = None
                for s in range(1, SPAN + 1):
                    if e >= SPAN - s:
                        flow = weight_ref[s - 1, quarter, e] * (p_ref[quarter, e + s] - here)
                        flows[s, e] = flow
                        if e >= SPAN:
                            term = flows.pop((s, e - s)) - flow
                            out = term if out is None else out + term
                if e >= SPAN:
                    out = out + DAMPING * here
                    q_ref[quarter, e - SPAN] = out
                    pq = pq + here * out
        a = rr / (over_dates(pq) + EPSILON)
        nn = zero
        for quarter in range(quarters):
            for u in range(dates):
                rows = pl.ds((quarter * dates + u) * 8, 8)
                x_ref[rows, :] = x_ref[rows, :] + a * p_ref[quarter, SPAN + u]
                rest = r_ref[quarter, u] - a * q_ref[quarter, u]
                r_ref[quarter, u] = rest
                nn = nn + rest * rest
        nn = over_dates(nn)
        ratio = nn / (rr + EPSILON)
        for quarter in range(quarters):
            for u in range(dates):
                p_ref[quarter, SPAN + u] = r_ref[quarter, u] + ratio * p_ref[quarter, SPAN + u]
        refresh_ghosts()
        return nn

    lax.fori_loop(0, ITERS, iteration, rr)
    for quarter in range(quarters):
        for j in range(4):
            for row in range(2):
                disp_ref[pl.ds((quarter * 4 + j) * 2 * dates + row, dates, stride=2), :] = x_ref[
                    pl.ds(quarter * dates * 8 + 2 * j + row, dates, stride=8), :
                ]
    copy.wait()


def vmem(count):
    return [pl.BlockSpec(memory_space=pltpu.VMEM)] * count


PARAMS = pltpu.CompilerParams(vmem_limit_bytes=48 * 1024 * 1024)


def shape(*sizes):
    return jax.ShapeDtypeStruct(sizes, F32)


def local(acquisitions, offsets):
    dates = acquisitions.shape[1]
    blocks = lax.axis_size("date")
    tiles = lax.axis_size("pix")
    near = dates - SPAN
    anywhere = [pl.BlockSpec(memory_space=pl.ANY)]
    offsets = offsets.T
    packed, kept, rim = pl.pallas_call(
        pack_kernel,
        out_shape=[
            shape(dates, 8, LANES), shape(2, dates, ROWS, LANES), shape(2, SPAN, ROWS, LANES),
        ],
        in_specs=vmem(1),
        out_specs=vmem(3),
        compiler_params=PARAMS,
    )(acquisitions)

    def moved(x, dates_back, tiles_on):
        route = [
            (p * blocks + d, (p + tiles_on) % tiles * blocks + (d - dates_back) % blocks)
            for p in range(tiles)
            for d in range(blocks)
        ]
        return lax.ppermute(x, ("pix", "date"), route)

    rim = moved(rim, 1, 0)
    left = moved(packed, 0, 1)
    right = moved(packed, 0, -1)

    sums, table = pl.pallas_call(
        functools.partial(center_kernel, near=near, batch=7),
        out_shape=[shape(2 * K * near + dates, ROWS, LANES), shape(K * dates + 1, 8, LANES)],
        in_specs=vmem(2),
        out_specs=vmem(2),
        compiler_params=PARAMS,
    )(offsets, kept)

    def corner_kernel(left_ref, right_ref, sums_ref, out_ref):
        del sums_ref
        for t in range(SPAN):
            out_ref[t] = edges(left_ref[t], right_ref[t])

    corner = pl.pallas_call(
        corner_kernel,
        out_shape=shape(SPAN, 8, LANES),
        in_specs=vmem(2) + anywhere,
        out_specs=vmem(1)[0],
        compiler_params=PARAMS,
    )(left, right, sums)
    corner = moved(corner, 1, 0)

    messages, halo, power, partial = pl.pallas_call(
        functools.partial(near_kernel, near=near, batch=7),
        out_shape=[
            shape(blocks * 2 * FIELDS, LANES),
            shape(dates, 8, LANES),
            shape(dates, ROWS, LANES),
            shape(SPAN, ROWS, LANES),
        ],
        in_specs=vmem(4),
        out_specs=vmem(4),
        scratch_shapes=[
            pltpu.VMEM((dates, 8, LANES), F32),
            pltpu.VMEM((dates, ROWS, LANES), F32),
        ],
        compiler_params=PARAMS,
    )(table, left, right, sums)

    far_sums = pl.pallas_call(
        functools.partial(far_center_kernel, near=near),
        out_shape=shape(SPAN + 2 * K * SPAN, ROWS, LANES),
        in_specs=vmem(3),
        out_specs=vmem(1)[0],
        compiler_params=PARAMS,
    )(table, kept, rim)

    messages = pl.pallas_call(
        functools.partial(far_kernel, near=near),
        out_shape=shape(blocks * 2 * FIELDS, LANES),
        in_specs=vmem(7),
        out_specs=vmem(1)[0],
        input_output_aliases={1: 0},
        scratch_shapes=[pltpu.VMEM((2 * SPAN, ROWS, LANES), F32)],
        compiler_params=PARAMS,
    )(table, messages, halo, corner, power, partial, far_sums)
    received = lax.all_to_all(messages, "date", split_axis=0, concat_axis=0, tiled=True)

    quarters = blocks // 4
    coherence, displacement = pl.pallas_call(
        functools.partial(solve_kernel, dates=dates),
        out_shape=[
            jax.ShapeDtypeStruct((blocks * dates * K * 2, LANES), F32),
            jax.ShapeDtypeStruct((blocks * dates * 2, LANES), F32),
        ],
        in_specs=vmem(1),
        out_specs=anywhere + vmem(1),
        scratch_shapes=[
            pltpu.VMEM((blocks * dates * K * 2, LANES), F32),
            pltpu.VMEM((SPAN, quarters, SPAN + dates, 8, LANES), F32),
            pltpu.VMEM((quarters, dates + 2 * SPAN, 8, LANES), F32),
            pltpu.VMEM((quarters, dates, 8, LANES), F32),
            pltpu.VMEM((quarters * dates * 8, LANES), F32),
            pltpu.VMEM((quarters, dates, 8, LANES), F32),
            pltpu.SemaphoreType.DMA,
        ],
        compiler_params=PARAMS,
    )(received)
    return (
        coherence.reshape(blocks * dates, K, 2, LANES),
        displacement.reshape(blocks * dates, 2, LANES),
    )


def solution(mesh):
    placed = (P(None, "date", None, "pix"), P("date", None))
    return jax.shard_map(
        local,
        mesh=mesh,
        in_specs=placed,
        out_specs=(P(None, None, "date", "pix"), P(None, "date", "pix")),
        check_vma=False,
    )
```

```python
import functools

import jax
import jax.numpy as jnp
from jax import lax
from jax.experimental import pallas as pl
from jax.experimental.pallas import tpu as pltpu
from jax.sharding import PartitionSpec as P

SPAN = 4
K = 3
HR = 2
HC = 7
ITERS = 6
DAMPING = 0.05
EPSILON = 1e-06

LANES = 128
ROWS = 32
GROUPS = ROWS // 8
FIELDS = 76
F32 = jnp.float32
BF16 = jnp.bfloat16


def lanes_of(shape):
    return lax.broadcasted_iota(jnp.int32, shape, len(shape) - 1)


def rows_of(shape):
    return lax.broadcasted_iota(jnp.int32, shape, len(shape) - 2)


def pack_kernel(acq_ref, packed_ref, kept_ref, rim_ref):
    lane = lanes_of((8, LANES))
    for t in range(acq_ref.shape[1]):
        total = jnp.zeros((8, LANES), F32)
        for f in range(2):
            for g in range(GROUPS):
                begin = 64 * f + 16 * g
                here = acq_ref[f, t, 8 * g : 8 * g + 8, :]
                kept_ref[f, t, 8 * g : 8 * g + 8, :] = here
                if t < SPAN:
                    rim_ref[f, t, 8 * g : 8 * g + 8, :] = here
                moved = pltpu.roll(here, begin + HC, 1)
                total = jnp.where((lane >= begin) & (lane < begin + 2 * HC), moved, total)
        packed_ref[t] = total


def edges(twin, other):
    tile, tiles = lax.axis_index("pix"), lax.axis_size("pix")
    lane = lanes_of(twin.shape) % 16
    low = jnp.where(tile == 0, HC, 0)
    high = jnp.where(tile == tiles - 1, HC, 2 * HC)
    both = jnp.where((lane < HC) == (tile % 2 == 1), twin, other)
    return jnp.where((lane >= low) & (lane < high), both, 0.0)


def halves(values):
    high = values.astype(BF16)
    return jnp.concatenate([high, (values - high.astype(F32)).astype(BF16)], axis=1)


def row_window(parts):
    sub = rows_of((8, LANES))
    zero = jnp.zeros((8, LANES), F32)

    def up(x, n, below):
        x = x + [below]
        return [pltpu.roll(jnp.where(sub >= n, x[g], x[g + 1]), 8 - n, 0) for g in range(GROUPS)]

    def down(x, n, above):
        x = [above] + x
        return [pltpu.roll(jnp.where(sub < 8 - n, x[g + 1], x[g]), n, 0) for g in range(GROUPS)]

    two = [a + b for a, b in zip(parts, up(parts, 1, zero))]
    above = jnp.where(sub == 7, pltpu.roll(parts[0], 7, 0), 0.0)
    return [a + b + c for a, b, c in zip(parts, up(two, 1, zero), down(two, 2, above))]


def packed_window(x):
    sub, place = rows_of((8, LANES)), lanes_of((8, LANES)) % 64
    below = jnp.where(place < 48, pltpu.roll(x, LANES - 16, 1), 0.0)
    above = jnp.where(place >= 16, pltpu.roll(x, 16, 1), 0.0)
    total = x
    for n in range(1, HR + 1):
        total = total + pltpu.roll(jnp.where(sub >= n, x, below), 8 - n, 0)
        total = total + pltpu.roll(jnp.where(sub < 8 - n, x, above), n, 0)
    return total


def center_band():
    row = lax.broadcasted_iota(jnp.int32, (LANES, LANES), 0)
    col = lax.broadcasted_iota(jnp.int32, (LANES, LANES), 1)
    band = (jnp.abs(row - col) <= HC).astype(F32).astype(BF16)
    return jnp.concatenate([band] * 2, axis=0)


def halo_band():
    row = lax.broadcasted_iota(jnp.int32, (LANES, LANES), 0)
    col = lax.broadcasted_iota(jnp.int32, (LANES, LANES), 1)
    place = row % 16
    reach = ((place < HC) & (col <= place)) | (
        (place >= HC) & (place < 2 * HC) & (col >= LANES - 2 * HC + place)
    )
    band = jnp.concatenate(
        [(reach & ((row % 64) // 16 == g)).astype(F32).astype(BF16) for g in range(GROUPS)], axis=1
    )
    return jnp.concatenate([band] * 2, axis=0)


def banded(fields, band):
    return jnp.dot(halves(jnp.concatenate(fields, axis=0)), band, preferred_element_type=F32)


def products(first, second):
    (re, im), (re2, im2) = first, second
    return [re * re2 + im * im2, im * re2 - re * im2]


def turn(halo):
    sign = jnp.where(lanes_of((8, LANES)) < 64, -1.0, 1.0).astype(F32)
    return pltpu.roll(halo, 64, 1) * sign


def center_windows(fields, band, out_ref, at):
    cols = banded(fields, band)
    for i in range(len(fields)):
        parts = [cols[ROWS * i + 8 * g : ROWS * i + 8 * g + 8] for g in range(GROUPS)]
        for g, part in enumerate(row_window(parts)):
            out_ref[at + i, 8 * g : 8 * g + 8, :] = part


def windows(center_ref, at, halos, band):
    rims = banded([packed_window(halo) for halo in halos], band)
    return [
        [
            center_ref[at + i, 8 * g : 8 * g + 8, :]
            + rims[8 * i : 8 * i + 8, LANES * g : LANES * (g + 1)]
            for g in range(GROUPS)
        ]
        for i in range(len(halos))
    ]


def chosen(offset, candidates):
    result = candidates[-1]
    for s in range(len(candidates) - 1, 0, -1):
        result = jnp.where(offset == float(s), candidates[s - 1], result)
    return result


def pair_fields(value, table_ref, dates):
    fields = []
    for t in dates:
        first = [[value(f, t, g) for f in range(2)] for g in range(GROUPS)]
        for k in range(K):
            offset = table_ref[K * t + k]
            pairs = [
                products(
                    first[g],
                    [
                        chosen(offset, [value(f, t + s, g) for s in range(1, SPAN + 1)])
                        for f in range(2)
                    ],
                )
                for g in range(GROUPS)
            ]
            fields += [jnp.concatenate([pair[c] for pair in pairs], axis=0) for c in range(2)]
    return fields


def power_fields(value, dates):
    fields = []
    for t in dates:
        parts = [[value(f, t, g) for f in range(2)] for g in range(GROUPS)]
        fields.append(jnp.concatenate([re * re + im * im for re, im in parts], axis=0))
    return fields


def center_kernel(off_ref, acq_ref, sums_ref, table_ref, *, near, batch):
    dates = acq_ref.shape[1]
    band = center_band()
    lane = lanes_of((8, LANES))
    row = jnp.zeros((8, LANES), F32)
    offsets = off_ref[...].astype(F32)
    for t in range(dates):
        for k in range(K):
            offset = jnp.broadcast_to(offsets[k : k + 1, t : t + 1], (8, LANES))
            table_ref[K * t + k] = offset
            row = jnp.where(lane == K * t + k, offset, row)
    table_ref[K * dates] = row

    def value(f, t, g):
        return acq_ref[f, t, 8 * g : 8 * g + 8, :]

    for begin in range(0, dates, dates // 2):
        fields = power_fields(value, range(begin, begin + dates // 2))
        center_windows(fields, band, sums_ref, 2 * K * near + begin)
    for begin in range(0, near, batch):
        fields = pair_fields(value, table_ref, range(begin, begin + batch))
        center_windows(fields, band, sums_ref, 2 * K * begin)


def far_center_kernel(table_ref, acq_ref, rim_ref, sums_ref, *, near):
    dates = acq_ref.shape[1]
    last = lax.axis_index("date") == lax.axis_size("date") - 1

    def value(f, t, g):
        rows = pl.ds(8 * g, 8)
        if t < dates:
            return acq_ref[f, t, rows, :]
        return jnp.where(last, 0.0, rim_ref[f, t - dates, rows, :])

    fields = power_fields(value, range(dates, dates + SPAN))
    fields += pair_fields(value, table_ref, range(near, dates))
    center_windows(fields, center_band(), sums_ref, 0)


def halo_pairs(table_ref, halo, turned, dates):
    fields = []
    for t in dates:
        for k in range(K):
            for field in (halo, turned):
                second = chosen(table_ref[K * t + k], [field(t + s) for s in range(1, SPAN + 1)])
                fields.append(halo(t) * second)
    return fields


def finish(looked, t, table_ref, power, limit, out_ref, add):
    offsets = [table_ref[K * t + k] for k in range(K)]
    for g in range(GROUPS):
        flows = []
        for k in range(K):
            re, im = looked[2 * k][g], looked[2 * k + 1][g]
            second = chosen(offsets[k], [power(t + s, g) for s in range(1, SPAN + 1)])
            scale = lax.rsqrt(power(t, g) * second + EPSILON)
            if limit is not None:
                scale = jnp.where(offsets[k] < limit, scale, 0.0)
            coherence = jnp.sqrt(re * re + im * im) * scale
            out_ref[pl.ds(8 * g * FIELDS + K * t + k, 8, stride=FIELDS), :] = coherence
            flows.append(coherence * (im * scale))
        total = flows[0]
        for flow in flows[1:]:
            total = total + flow
        add(t, g, -total)
        for s in range(1, SPAN + 1):
            share = jnp.zeros((8, LANES), F32)
            for offset, flow in zip(offsets, flows):
                share = jnp.where(offset == float(s), flow, share)
            add(t + s, g, share)


def near_kernel(
    table_ref, left_ref, right_ref, sums_ref,
    out_ref, halo_ref, power_ref, partial_ref, turned_ref, right_side_ref, *, near, batch,
):
    dates = left_ref.shape[0]
    band = halo_band()
    for t in range(dates):
        halo = edges(left_ref[t], right_ref[t])
        halo_ref[t] = halo
        turned_ref[t] = turn(halo)
        right_side_ref[t] = jnp.zeros((ROWS, LANES), F32)
    halos = [halo_ref[t] * halo_ref[t] for t in range(dates)]
    for t, parts in enumerate(windows(sums_ref, 2 * K * near, halos, band)):
        for g in range(GROUPS):
            power_ref[t, 8 * g : 8 * g + 8, :] = parts[g]

    def power(t, g):
        return power_ref[t, 8 * g : 8 * g + 8, :]

    def add(t, g, x):
        rows = pl.ds(8 * g, 8)
        right_side_ref[t, rows, :] = right_side_ref[t, rows, :] + x

    for begin in range(0, near, batch):
        group = range(begin, begin + batch)
        halos = halo_pairs(table_ref, lambda t: halo_ref[t], lambda t: turned_ref[t], group)
        looked = windows(sums_ref, 2 * K * begin, halos, band)
        for i, t in enumerate(group):
            finish(looked[2 * K * i : 2 * K * (i + 1)], t, table_ref, power, None, out_ref, add)
    for t in range(near):
        for g in range(GROUPS):
            out_ref[pl.ds(8 * g * FIELDS + K * dates + t, 8, stride=FIELDS), :] = right_side_ref[
                t, 8 * g : 8 * g + 8, :
            ]
    partial_ref[...] = right_side_ref[near:]


def far_kernel(
    table_ref, message_ref, near_halo_ref, corner_ref, near_power_ref, partial_ref, sums_ref,
    out_ref, right_side_ref, *, near,
):
    del message_ref
    dates = near_halo_ref.shape[0]
    total_dates = dates * lax.axis_size("date")
    first = lax.axis_index("date") * dates
    halo = {t: near_halo_ref[t] for t in range(near, dates)}
    for t in range(SPAN):
        halo[dates + t] = corner_ref[t]
        right_side_ref[t] = partial_ref[t]
        right_side_ref[SPAN + t] = jnp.zeros((ROWS, LANES), F32)
    turned = {t: turn(halo[t]) for t in halo}
    halos = [halo[t] * halo[t] for t in range(dates, dates + SPAN)]
    halos += halo_pairs(table_ref, lambda t: halo[t], lambda t: turned[t], range(near, dates))
    sums = windows(sums_ref, 0, halos, halo_band())

    def power(t, g):
        return sums[t - dates][g] if t >= dates else near_power_ref[t, 8 * g : 8 * g + 8, :]

    def add(t, g, x):
        rows = pl.ds(8 * g, 8)
        right_side_ref[t - near, rows, :] = right_side_ref[t - near, rows, :] + x

    for t in range(near, dates):
        n = SPAN + 2 * K * (t - near)
        limit = (total_dates - first - t).astype(F32)
        finish(sums[n : n + 2 * K], t, table_ref, power, limit, out_ref, add)
    for g in range(GROUPS):
        base = 8 * g * FIELDS + K * dates
        for t in range(near, dates + SPAN - 1):
            out_ref[pl.ds(base + t, 8, stride=FIELDS), :] = right_side_ref[
                t - near, 8 * g : 8 * g + 8, :
            ]
        out_ref[pl.ds(base + dates + SPAN - 1, 8, stride=FIELDS), :] = table_ref[K * dates]


def solve_kernel(
    recv_ref, coh_out, disp_out,
    coh_ref, disp_ref, weight_ref, p_ref, r_ref, x_ref, q_ref, sems, *, dates,
):
    quarters = recv_ref.shape[0] // (8 * FIELDS)
    chunk = 2 * FIELDS
    sub = rows_of((8, LANES))
    zero = jnp.zeros((8, LANES), F32)

    def received(quarter, f):
        return recv_ref[pl.ds(quarter * 8 * FIELDS + f, 8, stride=FIELDS), :]

    for d in range(4 * quarters):
        for row in range(2):
            coh_ref[pl.ds(d * 2 * K * dates + row, K * dates, stride=2), :] = recv_ref[
                pl.ds(d * chunk + row * FIELDS, K * dates), :
            ]
    copy = pltpu.make_async_copy(coh_ref, coh_out, sems.at[0])
    copy.start()

    def one_block_later(get, quarter):
        near = pltpu.roll(get(quarter), 6, 0)
        far = pltpu.roll(get(quarter + 1), 6, 0) if quarter + 1 < quarters else zero
        return jnp.where(sub < 6, near, far)

    def one_block_earlier(get, quarter):
        near = pltpu.roll(get(quarter), 2, 0)
        far = pltpu.roll(get(quarter - 1), 2, 0) if quarter > 0 else zero
        return jnp.where(sub >= 2, near, far)

    def over_dates(v):
        v = v + pltpu.roll(v, 4, 0)
        return v + pltpu.roll(v, 2, 0)

    def refresh_ghosts():
        for quarter in range(quarters):
            for e in range(SPAN):
                p_ref[quarter, SPAN + dates + e] = one_block_later(
                    lambda n: p_ref[n, SPAN + e], quarter
                )
                p_ref[quarter, e] = one_block_earlier(lambda n: p_ref[n, dates + e], quarter)

    rr = zero
    rims = []
    for quarter in range(quarters):
        rim = [received(quarter, K * dates + dates + e) for e in range(SPAN - 1)]
        rest = rim[0] + rim[1] + rim[2]
        for u in range(dates):
            rest = rest + received(quarter, K * dates + u)
        rims.append(rim + [-rest])
    for quarter in range(quarters):
        offsets = received(quarter, K * dates + dates + SPAN - 1)
        for u in range(dates):
            values = [received(quarter, K * u + k) for k in range(K)]
            places = [
                jnp.broadcast_to(offsets[:, K * u + k : K * u + k + 1], (8, LANES)) for k in range(K)
            ]
            for s in range(1, SPAN + 1):
                weight = zero
                for k in range(K):
                    weight = jnp.where(places[k] == float(s), values[k], weight)
                weight_ref[s - 1, quarter, SPAN + u] = weight
            b = received(quarter, K * dates + u)
            if u < SPAN:
                b = b + one_block_earlier(lambda n: rims[n][u], quarter)
            p_ref[quarter, SPAN + u] = b
            r_ref[quarter, u] = b
            x_ref[pl.ds((quarter * dates + u) * 8, 8), :] = zero
            rr = rr + b * b
    for quarter in range(quarters):
        for s in range(1, SPAN + 1):
            for e in range(SPAN - s, SPAN):
                weight_ref[s - 1, quarter, e] = one_block_earlier(
                    lambda n: weight_ref[s - 1, n, dates + e], quarter
                )
    rr = over_dates(rr)
    refresh_ghosts()

    def step_size(rr):
        pq = zero
        for quarter in range(quarters):
            flows = {}
            for e in range(dates + SPAN):
                here = p_ref[quarter, e]
                out = None
                for s in range(1, SPAN + 1):
                    if e >= SPAN - s:
                        flow = weight_ref[s - 1, quarter, e] * (p_ref[quarter, e + s] - here)
                        flows[s, e] = flow
                        if e >= SPAN:
                            term = flows.pop((s, e - s)) - flow
                            out = term if out is None else out + term
                if e >= SPAN:
                    out = out + DAMPING * here
                    q_ref[quarter, e - SPAN] = out
                    pq = pq + here * out
        return rr / (over_dates(pq) + EPSILON)

    def iteration(step, rr):
        a = step_size(rr)
        nn = zero
        for quarter in range(quarters):
            for u in range(dates):
                rows = pl.ds((quarter * dates + u) * 8, 8)
                x_ref[rows, :] = x_ref[rows, :] + a * p_ref[quarter, SPAN + u]
                rest = r_ref[quarter, u] - a * q_ref[quarter, u]
                r_ref[quarter, u] = rest
                nn = nn + rest * rest
        nn = over_dates(nn)
        ratio = nn / (rr + EPSILON)
        for quarter in range(quarters):
            for u in range(dates):
                p_ref[quarter, SPAN + u] = r_ref[quarter, u] + ratio * p_ref[quarter, SPAN + u]
        refresh_ghosts()
        return nn

    a = step_size(lax.fori_loop(0, ITERS - 1, iteration, rr))
    copies = [copy]
    for quarter in range(quarters):
        for u in range(dates):
            rows = pl.ds((quarter * dates + u) * 8, 8)
            x_ref[rows, :] = x_ref[rows, :] + a * p_ref[quarter, SPAN + u]
        for j in range(4):
            for row in range(2):
                disp_ref[pl.ds((quarter * 4 + j) * 2 * dates + row, dates, stride=2), :] = x_ref[
                    pl.ds(quarter * dates * 8 + 2 * j + row, dates, stride=8), :
                ]
        span = pl.ds(quarter * 8 * dates, 8 * dates)
        copies.append(
            pltpu.make_async_copy(disp_ref.at[span], disp_out.at[span], sems.at[1 + quarter])
        )
        copies[-1].start()
    for copy in copies:
        copy.wait()


def vmem(count):
    return [pl.BlockSpec(memory_space=pltpu.VMEM)] * count


PARAMS = pltpu.CompilerParams(vmem_limit_bytes=48 * 1024 * 1024)


def shape(*sizes):
    return jax.ShapeDtypeStruct(sizes, F32)


def local(acquisitions, offsets):
    dates = acquisitions.shape[1]
    blocks = lax.axis_size("date")
    tiles = lax.axis_size("pix")
    near = dates - SPAN
    anywhere = [pl.BlockSpec(memory_space=pl.ANY)]
    offsets = offsets.T
    packed, kept, rim = pl.pallas_call(
        pack_kernel,
        out_shape=[
            shape(dates, 8, LANES), shape(2, dates, ROWS, LANES), shape(2, SPAN, ROWS, LANES),
        ],
        in_specs=vmem(1),
        out_specs=vmem(3),
        compiler_params=PARAMS,
    )(acquisitions)

    def moved(x, partner, dates_back):
        route = []
        for p in range(tiles):
            for d in range(blocks):
                source = (d + dates_back) % blocks
                if partner(p) is None:
                    route.append((p * blocks + (source if dates_back else d ^ 1), p * blocks + d))
                else:
                    route.append((partner(p) * blocks + source, p * blocks + d))
        return lax.ppermute(x, ("pix", "date"), route)

    def same(p):
        return p

    def twin(p):
        return p ^ 1

    def other(p):
        return None if p in (0, tiles - 1) else p + 1 if p % 2 else p - 1

    rim = moved(rim, same, 1)
    left = moved(packed, twin, 0)
    right = moved(packed, other, 0)

    sums, table = pl.pallas_call(
        functools.partial(center_kernel, near=near, batch=7),
        out_shape=[shape(2 * K * near + dates, ROWS, LANES), shape(K * dates + 1, 8, LANES)],
        in_specs=vmem(2),
        out_specs=vmem(2),
        compiler_params=PARAMS,
    )(offsets, kept)

    def corner_kernel(left_ref, right_ref, sums_ref, out_ref):
        del sums_ref
        for t in range(SPAN):
            out_ref[t] = edges(left_ref[t], right_ref[t])

    corner = pl.pallas_call(
        corner_kernel,
        out_shape=shape(SPAN, 8, LANES),
        in_specs=vmem(2) + anywhere,
        out_specs=vmem(1)[0],
        compiler_params=PARAMS,
    )(left, right, sums)
    corner = moved(corner, same, 1)

    messages, halo, power, partial = pl.pallas_call(
        functools.partial(near_kernel, near=near, batch=7),
        out_shape=[
            shape(blocks * 2 * FIELDS, LANES),
            shape(dates, 8, LANES),
            shape(dates, ROWS, LANES),
            shape(SPAN, ROWS, LANES),
        ],
        in_specs=vmem(4),
        out_specs=vmem(4),
        scratch_shapes=[
            pltpu.VMEM((dates, 8, LANES), F32),
            pltpu.VMEM((dates, ROWS, LANES), F32),
        ],
        compiler_params=PARAMS,
    )(table, left, right, sums)

    far_sums = pl.pallas_call(
        functools.partial(far_center_kernel, near=near),
        out_shape=shape(SPAN + 2 * K * SPAN, ROWS, LANES),
        in_specs=vmem(3),
        out_specs=vmem(1)[0],
        compiler_params=PARAMS,
    )(table, kept, rim)

    messages = pl.pallas_call(
        functools.partial(far_kernel, near=near),
        out_shape=shape(blocks * 2 * FIELDS, LANES),
        in_specs=vmem(7),
        out_specs=vmem(1)[0],
        input_output_aliases={1: 0},
        scratch_shapes=[pltpu.VMEM((2 * SPAN, ROWS, LANES), F32)],
        compiler_params=PARAMS,
    )(table, messages, halo, corner, power, partial, far_sums)
    received = lax.all_to_all(messages, "date", split_axis=0, concat_axis=0, tiled=True)

    quarters = blocks // 4
    coherence, displacement = pl.pallas_call(
        functools.partial(solve_kernel, dates=dates),
        out_shape=[
            jax.ShapeDtypeStruct((blocks * dates * K * 2, LANES), F32),
            jax.ShapeDtypeStruct((blocks * dates * 2, LANES), F32),
        ],
        in_specs=vmem(1),
        out_specs=anywhere * 2,
        scratch_shapes=[
            pltpu.VMEM((blocks * dates * K * 2, LANES), F32),
            pltpu.VMEM((blocks * dates * 2, LANES), F32),
            pltpu.VMEM((SPAN, quarters, SPAN + dates, 8, LANES), F32),
            pltpu.VMEM((quarters, dates + 2 * SPAN, 8, LANES), F32),
            pltpu.VMEM((quarters, dates, 8, LANES), F32),
            pltpu.VMEM((quarters * dates * 8, LANES), F32),
            pltpu.VMEM((quarters, dates, 8, LANES), F32),
            pltpu.SemaphoreType.DMA((1 + quarters,)),
        ],
        compiler_params=PARAMS,
    )(received)
    return (
        coherence.reshape(blocks * dates, K, 2, LANES),
        displacement.reshape(blocks * dates, 2, LANES),
    )


def solution(mesh):
    placed = (P(None, "date", None, "pix"), P("date", None))
    return jax.shard_map(
        local,
        mesh=mesh,
        in_specs=placed,
        out_specs=(P(None, None, "date", "pix"), P(None, "date", "pix")),
        check_vma=False,
    )
```

```python
import functools

import jax
import jax.numpy as jnp
from jax import lax
from jax.experimental import pallas as pl
from jax.experimental.pallas import tpu as pltpu
from jax.sharding import PartitionSpec as P

SPAN = 4
K = 3
HR = 2
HC = 7
ITERS = 6
DAMPING = 0.05
EPSILON = 1e-06

LANES = 128
ROWS = 32
GROUPS = ROWS // 8
FIELDS = 76
F32 = jnp.float32
BF16 = jnp.bfloat16


def lanes_of(shape):
    return lax.broadcasted_iota(jnp.int32, shape, len(shape) - 1)


def rows_of(shape):
    return lax.broadcasted_iota(jnp.int32, shape, len(shape) - 2)


def pack_kernel(acq_ref, packed_ref, kept_ref, rim_ref):
    lane = lanes_of((8, LANES))
    for t in range(acq_ref.shape[1]):
        total = jnp.zeros((8, LANES), F32)
        for f in range(2):
            for g in range(GROUPS):
                begin = 64 * f + 16 * g
                here = acq_ref[f, t, 8 * g : 8 * g + 8, :]
                kept_ref[f, t, 8 * g : 8 * g + 8, :] = here
                if t < SPAN:
                    rim_ref[f, t, 8 * g : 8 * g + 8, :] = here
                moved = pltpu.roll(here, begin + HC, 1)
                total = jnp.where((lane >= begin) & (lane < begin + 2 * HC), moved, total)
        packed_ref[t] = total


def edges(twin, other):
    tile, tiles = lax.axis_index("pix"), lax.axis_size("pix")
    lane = lanes_of(twin.shape) % 16
    low = jnp.where(tile == 0, HC, 0)
    high = jnp.where(tile == tiles - 1, HC, 2 * HC)
    both = jnp.where((lane < HC) == (tile % 2 == 1), twin, other)
    return jnp.where((lane >= low) & (lane < high), both, 0.0)


def halves(values):
    high = values.astype(BF16)
    return jnp.concatenate([high, (values - high.astype(F32)).astype(BF16)], axis=1)


def row_window(parts):
    sub = rows_of((8, LANES))
    zero = jnp.zeros((8, LANES), F32)

    def up(x, n, below):
        x = x + [below]
        return [pltpu.roll(jnp.where(sub >= n, x[g], x[g + 1]), 8 - n, 0) for g in range(GROUPS)]

    def down(x, n, above):
        x = [above] + x
        return [pltpu.roll(jnp.where(sub < 8 - n, x[g + 1], x[g]), n, 0) for g in range(GROUPS)]

    two = [a + b for a, b in zip(parts, up(parts, 1, zero))]
    above = jnp.where(sub == 7, pltpu.roll(parts[0], 7, 0), 0.0)
    return [a + b + c for a, b, c in zip(parts, up(two, 1, zero), down(two, 2, above))]


def packed_window(x):
    sub, place = rows_of((8, LANES)), lanes_of((8, LANES)) % 64
    below = jnp.where(place < 48, pltpu.roll(x, LANES - 16, 1), 0.0)
    above = jnp.where(place >= 16, pltpu.roll(x, 16, 1), 0.0)
    total = x
    for n in range(1, HR + 1):
        total = total + pltpu.roll(jnp.where(sub >= n, x, below), 8 - n, 0)
        total = total + pltpu.roll(jnp.where(sub < 8 - n, x, above), n, 0)
    return total


def center_band():
    row = lax.broadcasted_iota(jnp.int32, (LANES, LANES), 0)
    col = lax.broadcasted_iota(jnp.int32, (LANES, LANES), 1)
    band = (jnp.abs(row - col) <= HC).astype(F32).astype(BF16)
    return jnp.concatenate([band] * 2, axis=0)


def halo_band():
    row = lax.broadcasted_iota(jnp.int32, (LANES, LANES), 0)
    col = lax.broadcasted_iota(jnp.int32, (LANES, LANES), 1)
    place = row % 16
    reach = ((place < HC) & (col <= place)) | (
        (place >= HC) & (place < 2 * HC) & (col >= LANES - 2 * HC + place)
    )
    band = jnp.concatenate(
        [(reach & ((row % 64) // 16 == g)).astype(F32).astype(BF16) for g in range(GROUPS)], axis=1
    )
    return jnp.concatenate([band] * 2, axis=0)


def banded(fields, band):
    return jnp.dot(halves(jnp.concatenate(fields, axis=0)), band, preferred_element_type=F32)


def products(first, second):
    (re, im), (re2, im2) = first, second
    return [re * re2 + im * im2, im * re2 - re * im2]


def turn(halo):
    sign = jnp.where(lanes_of((8, LANES)) < 64, -1.0, 1.0).astype(F32)
    return pltpu.roll(halo, 64, 1) * sign


def center_windows(fields, band, out_ref, at):
    cols = banded(fields, band)
    for i in range(len(fields)):
        parts = [cols[ROWS * i + 8 * g : ROWS * i + 8 * g + 8] for g in range(GROUPS)]
        for g, part in enumerate(row_window(parts)):
            out_ref[at + i, 8 * g : 8 * g + 8, :] = part


def windows(center_ref, at, halos, band):
    rims = banded([packed_window(halo) for halo in halos], band)
    return [
        [
            center_ref[at + i, 8 * g : 8 * g + 8, :]
            + rims[8 * i : 8 * i + 8, LANES * g : LANES * (g + 1)]
            for g in range(GROUPS)
        ]
        for i in range(len(halos))
    ]


def chosen(offset, candidates):
    result = candidates[-1]
    for s in range(len(candidates) - 1, 0, -1):
        result = jnp.where(offset == float(s), candidates[s - 1], result)
    return result


def pair_fields(value, table_ref, dates):
    fields = []
    for t in dates:
        first = [[value(f, t, g) for f in range(2)] for g in range(GROUPS)]
        for k in range(K):
            offset = table_ref[K * t + k]
            pairs = [
                products(
                    first[g],
                    [
                        chosen(offset, [value(f, t + s, g) for s in range(1, SPAN + 1)])
                        for f in range(2)
                    ],
                )
                for g in range(GROUPS)
            ]
            fields += [jnp.concatenate([pair[c] for pair in pairs], axis=0) for c in range(2)]
    return fields


def power_fields(value, dates):
    fields = []
    for t in dates:
        parts = [[value(f, t, g) for f in range(2)] for g in range(GROUPS)]
        fields.append(jnp.concatenate([re * re + im * im for re, im in parts], axis=0))
    return fields


def center_kernel(off_ref, acq_ref, sums_ref, table_ref, *, near, batch):
    dates = acq_ref.shape[1]
    band = center_band()
    lane = lanes_of((8, LANES))
    row = jnp.zeros((8, LANES), F32)
    offsets = off_ref[...].astype(F32)
    for t in range(dates):
        for k in range(K):
            offset = jnp.broadcast_to(offsets[k : k + 1, t : t + 1], (8, LANES))
            table_ref[K * t + k] = offset
            row = jnp.where(lane == K * t + k, offset, row)
    table_ref[K * dates] = row

    def value(f, t, g):
        return acq_ref[f, t, 8 * g : 8 * g + 8, :]

    for begin in range(0, dates, dates // 2):
        fields = power_fields(value, range(begin, begin + dates // 2))
        center_windows(fields, band, sums_ref, 2 * K * near + begin)
    for begin in range(0, near, batch):
        fields = pair_fields(value, table_ref, range(begin, begin + batch))
        center_windows(fields, band, sums_ref, 2 * K * begin)


def far_center_kernel(table_ref, acq_ref, rim_ref, sums_ref, *, near):
    dates = acq_ref.shape[1]
    last = lax.axis_index("date") == lax.axis_size("date") - 1

    def value(f, t, g):
        rows = pl.ds(8 * g, 8)
        if t < dates:
            return acq_ref[f, t, rows, :]
        return jnp.where(last, 0.0, rim_ref[f, t - dates, rows, :])

    fields = power_fields(value, range(dates, dates + SPAN))
    fields += pair_fields(value, table_ref, range(near, dates))
    center_windows(fields, center_band(), sums_ref, 0)


def halo_pairs(table_ref, halo, turned, dates):
    fields = []
    for t in dates:
        for k in range(K):
            for field in (halo, turned):
                second = chosen(table_ref[K * t + k], [field(t + s) for s in range(1, SPAN + 1)])
                fields.append(halo(t) * second)
    return fields


def finish(looked, t, table_ref, power, limit, out_ref, add):
    offsets = [table_ref[K * t + k] for k in range(K)]
    for g in range(GROUPS):
        flows = []
        for k in range(K):
            re, im = looked[2 * k][g], looked[2 * k + 1][g]
            second = chosen(offsets[k], [power(t + s, g) for s in range(1, SPAN + 1)])
            scale = lax.rsqrt(power(t, g) * second + EPSILON)
            if limit is not None:
                scale = jnp.where(offsets[k] < limit, scale, 0.0)
            coherence = jnp.sqrt(re * re + im * im) * scale
            out_ref[pl.ds(8 * g * FIELDS + K * t + k, 8, stride=FIELDS), :] = coherence
            flows.append(coherence * (im * scale))
        total = flows[0]
        for flow in flows[1:]:
            total = total + flow
        add(t, g, -total)
        for s in range(1, SPAN + 1):
            share = jnp.zeros((8, LANES), F32)
            for offset, flow in zip(offsets, flows):
                share = jnp.where(offset == float(s), flow, share)
            add(t + s, g, share)


def near_kernel(
    table_ref, left_ref, right_ref, sums_ref,
    out_ref, halo_ref, power_ref, partial_ref, turned_ref, right_side_ref, *, near, batch,
):
    dates = left_ref.shape[0]
    band = halo_band()
    for t in range(dates):
        halo = edges(left_ref[t], right_ref[t])
        halo_ref[t] = halo
        turned_ref[t] = turn(halo)
        right_side_ref[t] = jnp.zeros((ROWS, LANES), F32)
    halos = [halo_ref[t] * halo_ref[t] for t in range(dates)]
    for t, parts in enumerate(windows(sums_ref, 2 * K * near, halos, band)):
        for g in range(GROUPS):
            power_ref[t, 8 * g : 8 * g + 8, :] = parts[g]

    def power(t, g):
        return power_ref[t, 8 * g : 8 * g + 8, :]

    def add(t, g, x):
        rows = pl.ds(8 * g, 8)
        right_side_ref[t, rows, :] = right_side_ref[t, rows, :] + x

    for begin in range(0, near, batch):
        group = range(begin, begin + batch)
        halos = halo_pairs(table_ref, lambda t: halo_ref[t], lambda t: turned_ref[t], group)
        looked = windows(sums_ref, 2 * K * begin, halos, band)
        for i, t in enumerate(group):
            finish(looked[2 * K * i : 2 * K * (i + 1)], t, table_ref, power, None, out_ref, add)
    for t in range(near):
        for g in range(GROUPS):
            out_ref[pl.ds(8 * g * FIELDS + K * dates + t, 8, stride=FIELDS), :] = right_side_ref[
                t, 8 * g : 8 * g + 8, :
            ]
    partial_ref[...] = right_side_ref[near:]


def far_kernel(
    table_ref, message_ref, near_halo_ref, corner_ref, near_power_ref, partial_ref, sums_ref,
    out_ref, right_side_ref, *, near,
):
    del message_ref
    dates = near_halo_ref.shape[0]
    total_dates = dates * lax.axis_size("date")
    first = lax.axis_index("date") * dates
    halo = {t: near_halo_ref[t] for t in range(near, dates)}
    for t in range(SPAN):
        halo[dates + t] = corner_ref[t]
        right_side_ref[t] = partial_ref[t]
        right_side_ref[SPAN + t] = jnp.zeros((ROWS, LANES), F32)
    turned = {t: turn(halo[t]) for t in halo}
    halos = [halo[t] * halo[t] for t in range(dates, dates + SPAN)]
    halos += halo_pairs(table_ref, lambda t: halo[t], lambda t: turned[t], range(near, dates))
    sums = windows(sums_ref, 0, halos, halo_band())

    def power(t, g):
        return sums[t - dates][g] if t >= dates else near_power_ref[t, 8 * g : 8 * g + 8, :]

    def add(t, g, x):
        rows = pl.ds(8 * g, 8)
        right_side_ref[t - near, rows, :] = right_side_ref[t - near, rows, :] + x

    for t in range(near, dates):
        n = SPAN + 2 * K * (t - near)
        limit = (total_dates - first - t).astype(F32)
        finish(sums[n : n + 2 * K], t, table_ref, power, limit, out_ref, add)
    for g in range(GROUPS):
        base = 8 * g * FIELDS + K * dates
        for t in range(near, dates + SPAN - 1):
            out_ref[pl.ds(base + t, 8, stride=FIELDS), :] = right_side_ref[
                t - near, 8 * g : 8 * g + 8, :
            ]
        out_ref[pl.ds(base + dates + SPAN - 1, 8, stride=FIELDS), :] = table_ref[K * dates]


def solve_kernel(
    recv_ref, coh_out, disp_out,
    coh_ref, disp_ref, weight_ref, p_ref, r_ref, x_ref, q_ref, sems, *, dates,
):
    quarters = recv_ref.shape[0] // (8 * FIELDS)
    chunk = 2 * FIELDS
    sub = rows_of((8, LANES))
    zero = jnp.zeros((8, LANES), F32)

    def received(quarter, f):
        return recv_ref[pl.ds(quarter * 8 * FIELDS + f, 8, stride=FIELDS), :]

    for d in range(4 * quarters):
        for row in range(2):
            coh_ref[pl.ds(d * 2 * K * dates + row, K * dates, stride=2), :] = recv_ref[
                pl.ds(d * chunk + row * FIELDS, K * dates), :
            ]
    copy = pltpu.make_async_copy(coh_ref, coh_out, sems.at[0])
    copy.start()

    def one_block_later(get, quarter):
        near = pltpu.roll(get(quarter), 6, 0)
        far = pltpu.roll(get(quarter + 1), 6, 0) if quarter + 1 < quarters else zero
        return jnp.where(sub < 6, near, far)

    def one_block_earlier(get, quarter):
        near = pltpu.roll(get(quarter), 2, 0)
        far = pltpu.roll(get(quarter - 1), 2, 0) if quarter > 0 else zero
        return jnp.where(sub >= 2, near, far)

    def over_dates(v):
        v = v + pltpu.roll(v, 4, 0)
        return v + pltpu.roll(v, 2, 0)

    def refresh_ghosts():
        for quarter in range(quarters):
            for e in range(SPAN):
                p_ref[quarter, SPAN + dates + e] = one_block_later(
                    lambda n: p_ref[n, SPAN + e], quarter
                )
                p_ref[quarter, e] = one_block_earlier(lambda n: p_ref[n, dates + e], quarter)

    rr = zero
    rims = []
    for quarter in range(quarters):
        rim = [received(quarter, K * dates + dates + e) for e in range(SPAN - 1)]
        rest = rim[0] + rim[1] + rim[2]
        for u in range(dates):
            rest = rest + received(quarter, K * dates + u)
        rims.append(rim + [-rest])
    for quarter in range(quarters):
        offsets = received(quarter, K * dates + dates + SPAN - 1)
        for u in range(dates):
            values = [received(quarter, K * u + k) for k in range(K)]
            places = [
                jnp.broadcast_to(offsets[:, K * u + k : K * u + k + 1], (8, LANES)) for k in range(K)
            ]
            for s in range(1, SPAN + 1):
                weight = zero
                for k in range(K):
                    weight = jnp.where(places[k] == float(s), values[k], weight)
                weight_ref[s - 1, quarter, SPAN + u] = weight
            b = received(quarter, K * dates + u)
            if u < SPAN:
                b = b + one_block_earlier(lambda n: rims[n][u], quarter)
            p_ref[quarter, SPAN + u] = b
            r_ref[quarter, u] = b
            x_ref[pl.ds((quarter * dates + u) * 8, 8), :] = zero
            rr = rr + b * b
    for quarter in range(quarters):
        for s in range(1, SPAN + 1):
            for e in range(SPAN - s, SPAN):
                weight_ref[s - 1, quarter, e] = one_block_earlier(
                    lambda n: weight_ref[s - 1, n, dates + e], quarter
                )
    rr = over_dates(rr)
    refresh_ghosts()

    def step_size(rr):
        pq = zero
        for quarter in range(quarters):
            flows = {}
            for e in range(dates + SPAN):
                here = p_ref[quarter, e]
                out = None
                for s in range(1, SPAN + 1):
                    if e >= SPAN - s:
                        flow = weight_ref[s - 1, quarter, e] * (p_ref[quarter, e + s] - here)
                        flows[s, e] = flow
                        if e >= SPAN:
                            term = flows.pop((s, e - s)) - flow
                            out = term if out is None else out + term
                if e >= SPAN:
                    out = out + DAMPING * here
                    q_ref[quarter, e - SPAN] = out
                    pq = pq + here * out
        return rr / (over_dates(pq) + EPSILON)

    def iteration(step, rr):
        a = step_size(rr)
        nn = zero
        for quarter in range(quarters):
            for u in range(dates):
                rows = pl.ds((quarter * dates + u) * 8, 8)
                x_ref[rows, :] = x_ref[rows, :] + a * p_ref[quarter, SPAN + u]
                rest = r_ref[quarter, u] - a * q_ref[quarter, u]
                r_ref[quarter, u] = rest
                nn = nn + rest * rest
        nn = over_dates(nn)
        ratio = nn / (rr + EPSILON)
        for quarter in range(quarters):
            for u in range(dates):
                p_ref[quarter, SPAN + u] = r_ref[quarter, u] + ratio * p_ref[quarter, SPAN + u]
        refresh_ghosts()
        return nn

    a = step_size(lax.fori_loop(0, ITERS - 1, iteration, rr))
    copies = [copy]
    for quarter in range(quarters):
        for u in range(dates):
            rows = pl.ds((quarter * dates + u) * 8, 8)
            x_ref[rows, :] = x_ref[rows, :] + a * p_ref[quarter, SPAN + u]
        for j in range(4):
            for row in range(2):
                disp_ref[pl.ds((quarter * 4 + j) * 2 * dates + row, dates, stride=2), :] = x_ref[
                    pl.ds(quarter * dates * 8 + 2 * j + row, dates, stride=8), :
                ]
        span = pl.ds(quarter * 8 * dates, 8 * dates)
        copies.append(
            pltpu.make_async_copy(disp_ref.at[span], disp_out.at[span], sems.at[1 + quarter])
        )
        copies[-1].start()
    for copy in copies:
        copy.wait()


def vmem(count):
    return [pl.BlockSpec(memory_space=pltpu.VMEM)] * count


PARAMS = pltpu.CompilerParams(vmem_limit_bytes=48 * 1024 * 1024)


def shape(*sizes):
    return jax.ShapeDtypeStruct(sizes, F32)


def local(acquisitions, offsets):
    dates = acquisitions.shape[1]
    blocks = lax.axis_size("date")
    tiles = lax.axis_size("pix")
    near = dates - SPAN
    anywhere = [pl.BlockSpec(memory_space=pl.ANY)]
    offsets = offsets.T
    packed, kept, rim = pl.pallas_call(
        pack_kernel,
        out_shape=[
            shape(dates, 8, LANES), shape(2, dates, ROWS, LANES), shape(2, SPAN, ROWS, LANES),
        ],
        in_specs=vmem(1),
        out_specs=vmem(3),
        compiler_params=PARAMS,
    )(acquisitions)

    def moved(x, partner, dates_back):
        route = []
        for p in range(tiles):
            for d in range(blocks):
                source = (d + dates_back) % blocks
                if partner(p) is None:
                    route.append((p * blocks + (source if dates_back else d ^ 1), p * blocks + d))
                else:
                    route.append((partner(p) * blocks + source, p * blocks + d))
        return lax.ppermute(x, ("pix", "date"), route)

    def same(p):
        return p

    def twin(p):
        return p ^ 1

    def other(p):
        return None if p in (0, tiles - 1) else p + 1 if p % 2 else p - 1

    rim = moved(rim, same, 1)
    left = moved(packed, twin, 0)
    right = moved(packed, other, 0)

    sums, table = pl.pallas_call(
        functools.partial(center_kernel, near=near, batch=7),
        out_shape=[shape(2 * K * near + dates, ROWS, LANES), shape(K * dates + 1, 8, LANES)],
        in_specs=vmem(2),
        out_specs=vmem(2),
        compiler_params=PARAMS,
        cost_estimate=pl.CostEstimate(flops=20000000000, transcendentals=0, bytes_accessed=60000000),
    )(offsets, kept)

    def corner_kernel(left_ref, right_ref, sums_ref, out_ref):
        del sums_ref
        for t in range(SPAN):
            out_ref[t] = edges(left_ref[t], right_ref[t])

    corner = pl.pallas_call(
        corner_kernel,
        out_shape=shape(SPAN, 8, LANES),
        in_specs=vmem(2) + anywhere,
        out_specs=vmem(1)[0],
        compiler_params=PARAMS,
        cost_estimate=pl.CostEstimate(flops=10000000, transcendentals=0, bytes_accessed=30000),
    )(left, right, sums)
    corner = moved(corner, same, 1)

    messages, halo, power, partial = pl.pallas_call(
        functools.partial(near_kernel, near=near, batch=7),
        out_shape=[
            shape(blocks * 2 * FIELDS, LANES),
            shape(dates, 8, LANES),
            shape(dates, ROWS, LANES),
            shape(SPAN, ROWS, LANES),
        ],
        in_specs=vmem(4),
        out_specs=vmem(4),
        scratch_shapes=[
            pltpu.VMEM((dates, 8, LANES), F32),
            pltpu.VMEM((dates, ROWS, LANES), F32),
        ],
        compiler_params=PARAMS,
        cost_estimate=pl.CostEstimate(flops=20000000000, transcendentals=0, bytes_accessed=60000000),
    )(table, left, right, sums)

    far_sums = pl.pallas_call(
        functools.partial(far_center_kernel, near=near),
        out_shape=shape(SPAN + 2 * K * SPAN, ROWS, LANES),
        in_specs=vmem(3),
        out_specs=vmem(1)[0],
        compiler_params=PARAMS,
        cost_estimate=pl.CostEstimate(flops=1000000000, transcendentals=0, bytes_accessed=3000000),
    )(table, kept, rim)

    messages = pl.pallas_call(
        functools.partial(far_kernel, near=near),
        out_shape=shape(blocks * 2 * FIELDS, LANES),
        in_specs=vmem(7),
        out_specs=vmem(1)[0],
        input_output_aliases={1: 0},
        scratch_shapes=[pltpu.VMEM((2 * SPAN, ROWS, LANES), F32)],
        compiler_params=PARAMS,
        cost_estimate=pl.CostEstimate(flops=1000000000, transcendentals=0, bytes_accessed=3000000),
    )(table, messages, halo, corner, power, partial, far_sums)
    received = lax.all_to_all(messages, "date", split_axis=0, concat_axis=0, tiled=True)

    quarters = blocks // 4
    coherence, displacement = pl.pallas_call(
        functools.partial(solve_kernel, dates=dates),
        out_shape=[
            jax.ShapeDtypeStruct((blocks * dates * K * 2, LANES), F32),
            jax.ShapeDtypeStruct((blocks * dates * 2, LANES), F32),
        ],
        in_specs=vmem(1),
        out_specs=anywhere * 2,
        scratch_shapes=[
            pltpu.VMEM((blocks * dates * K * 2, LANES), F32),
            pltpu.VMEM((blocks * dates * 2, LANES), F32),
            pltpu.VMEM((SPAN, quarters, SPAN + dates, 8, LANES), F32),
            pltpu.VMEM((quarters, dates + 2 * SPAN, 8, LANES), F32),
            pltpu.VMEM((quarters, dates, 8, LANES), F32),
            pltpu.VMEM((quarters * dates * 8, LANES), F32),
            pltpu.VMEM((quarters, dates, 8, LANES), F32),
            pltpu.SemaphoreType.DMA((1 + quarters,)),
        ],
        compiler_params=PARAMS,
        cost_estimate=pl.CostEstimate(flops=1000000000, transcendentals=0, bytes_accessed=3000000),
    )(received)
    return (
        coherence.reshape(blocks * dates, K, 2, LANES),
        displacement.reshape(blocks * dates, 2, LANES),
    )


def solution(mesh):
    placed = (P(None, "date", None, "pix"), P("date", None))
    return jax.shard_map(
        local,
        mesh=mesh,
        in_specs=placed,
        out_specs=(P(None, None, "date", "pix"), P(None, "date", "pix")),
        check_vma=False,
    )
```
